32 devices in a mesh: dp: 2 (over core), mp: 16 (over z, y, x).
Axes of the slice: x: 2, y: 2, z: 4, core: 2. Of those that a mesh axis runs over, the one named last changes fastest.
Arguments:
- queries: bfloat16 [4096, 768], P(('dp', 'mp')), may hold values from -30 to 30
- first_owner: int32 [4096, 1], P(('dp', 'mp')), may hold values from 0 to 15; in each aligned block of 128 rows (0 to 127, 128 to 255, ...) at most 16 rows name the same one
- first_row: int32 [4096], P(('dp', 'mp')), may hold values from 0 to 255
- tool_table: bfloat16 [4096, 768], P('mp'), may hold values from -6 to 6
- norm_gain: bfloat16 [768], replicated, may hold values from 0.25 to 1.75
- weight_in: bfloat16 [3072, 768], P('mp'), may hold values from -0.21875 to 0.21875
- bias_in: bfloat16 [3072], P('mp'), may hold values from -3 to 3
- weight_out: bfloat16 [3072, 768], P('mp'), may hold values from -0.109375 to 0.109375
- bias_out: bfloat16 [768], replicated, may hold values from -3 to 3
- tool_embeds: bfloat16 [128, 768], P('dp'), may hold values from -2 to 2
- positive: int32 [4096], P(('dp', 'mp')), may hold values from 0 to 127
Outputs:
- updated: bfloat16 [4096, 768], P(('dp', 'mp'))
- chain_loss: float32 [4096], P(('dp', 'mp'))
- query_grad: float32 [4096, 768], P(('dp', 'mp'))
- tool_grad: float32 [128, 768], P('dp')
The draws below stay inside these ranges and needn't reach their ends.
Inputs may be any that keep to these rules, and one draw needn't show every extreme that they name: `first_owner`: among the 128 chains of one device at most 16 name the same owner, a bound that some block reaches of them.
All inputs are finite; a program needn't handle non-finite values.
Results may differ from the reference program's by a relative error of at most 0.0078.
Values may be sent and summed in bfloat16 or wider, within the bound.
No kernel may reach another device: no remote copies, remote signals or barrier semaphores. Data moves between devices by JAX's collectives and lax.ppermute only.
A program may use at most 64 MiB of HBM per device.

```python
import math
import jax
import jax.numpy as jnp
import numpy as np
from jax import lax

D = 768
H = 3072
CH_DEV = 128
ROWS_OWN = 256
CAP = 16
CHAINS = 4096
TB = 128
TOOLS = 4096
N_MP = 16


def draw_queries(key, part):
    noise_key, scale_key = jax.random.split(jax.random.fold_in(key, 11))
    row_scale = jnp.exp(jax.random.uniform(scale_key, (CHAINS, 1), jnp.float32, math.log(0.5), math.log(5.0)))
    values = jnp.clip(jax.random.normal(noise_key, (CHAINS, D), jnp.float32), -6.0, 6.0) * row_scale
    return values.astype(jnp.bfloat16)


def draw_tool_embeds(key, part):
    noise_key, scale_key = jax.random.split(jax.random.fold_in(key, 23))
    row_scale = jnp.exp(jax.random.uniform(scale_key, (TB, 1), jnp.float32, math.log(0.4), math.log(4.0))) / math.sqrt(D)
    values = jnp.clip(jax.random.normal(noise_key, (TB, D), jnp.float32), -6.0, 6.0) * row_scale
    return values.astype(jnp.bfloat16)


def place_ends(values, own_key, least, largest):
    shape = values.shape
    place = [jax.random.randint(jax.random.fold_in(own_key, axis), (), 0, shape[axis]) for axis in range(len(shape))]
    values = values.at[tuple(place)].set(least)
    longest = shape.index(max(shape))
    place[longest] = (place[longest] + 1) % shape[longest]
    return values.at[tuple(place)].set(largest)


def steps_of(stream_key, shape, shards, least, largest):
    factor_of = 1.0
    for position, parts in shards:
        heights = jax.random.uniform(jax.random.fold_in(jax.random.fold_in(stream_key, 6), position), (parts,), jnp.float32, least / len(shards), largest / len(shards))
        factor_of = factor_of * jnp.repeat(jnp.exp(heights), shape[position] // parts).reshape((-1,) + (1,) * (len(shape) - 1 - position))
    return factor_of


def shared_out(rng, own, number, rows, amount, top, most, lean):
    ranking = jax.random.permutation(rng, amount)
    crowded, common = load_shares(amount, rows * top, most, lean, True), load_shares(amount, rows * top, most, lean, False)
    places = jnp.arange(amount)

    def named(lengths, offset_by):
        used = int((lengths > 0).sum())
        fixed = max(1, used // 4)
        shifted = fixed + (places - fixed + offset_by * (used - fixed)) % max(1, amount - fixed)
        return jnp.zeros((amount,), jnp.int32).at[ranking[jnp.where(places < fixed, places, shifted)]].set(jnp.asarray(lengths, jnp.int32))

    lengths = jnp.where(number % 4 == 0, named(crowded, number // 4), named(common, number - number // 4 - 1))
    mixed = jax.random.permutation(jax.random.fold_in(own, 3), amount)
    giver, receiver = mixed[0:amount // 2 * 2:2], mixed[1:amount // 2 * 2:2]
    room = jnp.minimum(lengths[giver] - 1, most - lengths[receiver]) // 2
    room = jnp.where((giver == ranking[0]) | (receiver == ranking[0]) | (lengths[receiver] == 0), 0, jnp.maximum(room, 0))
    shifted = jax.random.randint(jax.random.fold_in(own, 4), (amount // 2,), 0, 1 << 20) % (room + 1)
    lengths = lengths.at[giver].add(-shifted).at[receiver].add(shifted)
    items = jnp.searchsorted(jnp.cumsum(lengths), jnp.arange(rows * top), side="right").astype(jnp.int32)
    listing = items.reshape(top, rows).T
    listing = listing[jax.random.permutation(jax.random.fold_in(own, 1), rows)]
    offset_by = jax.random.randint(jax.random.fold_in(own, 2), (rows, 1), 0, top)
    return jnp.take_along_axis(listing, (jnp.arange(top)[None, :] + offset_by) % top, axis=1)


def load_shares(amount, total, bound, skew, full):
    loads = [(1 << 20) // math.isqrt(grade ** skew) + 1 for grade in range(1, amount + 1)]
    largest = bound if full else min(bound, max(-(-total // amount), total * loads[0] // sum(loads)))
    least = 1 if total - largest >= amount - 1 else 0
    given, rest = [largest] + [least] * (amount - 1), total - largest - least * (amount - 1)
    while rest > 0:
        candidates = [i for i in range(1, amount) if given[i] < largest] or [i for i in range(1, amount) if given[i] < bound]
        whole, remaining = sum([loads[i] for i in candidates]), rest
        for i in candidates:
            more = min(bound - given[i], max(1, remaining * loads[i] // whole), rest)
            given[i] = given[i] + more
            rest = rest - more
    return np.array(given)


def bell_draw(own_key, extent, width, most, shards=(), held_as=jnp.bfloat16):
    result = jax.random.normal(own_key, extent, jnp.float32) * width
    if len(shards) > 0:
        result = steps_of(own_key, extent, shards, -0.22, 0.18) * result
    return jnp.clip(result, min=-most, max=most).astype(held_as)


def setup_inputs(seed: int = 0) -> dict:
    keys = jax.random.split(jax.random.key(seed), 12)
    queries = draw_queries(jax.random.fold_in(keys[11], 71), 0)
    first_owner_keys = jax.random.split(jax.random.fold_in(keys[1], 1), CHAINS // CH_DEV)
    first_owner_turns = jax.random.permutation(jax.random.fold_in(keys[1], 3), CHAINS // CH_DEV)
    first_owner = jax.vmap(lambda own, number: shared_out(jax.random.fold_in(keys[1], 2), own, number, CH_DEV, N_MP, 1, CAP, 2))(first_owner_keys, first_owner_turns).reshape((CHAINS, 1))
    first_row = place_ends(jax.random.randint(keys[2], (CHAINS,), 0, ROWS_OWN), jax.random.fold_in(keys[2], 1), 0, ROWS_OWN - 1).astype(jnp.int32)
    tool_table = bell_draw(keys[3], (TOOLS, D), 1.0, 6.0, ((0, 16),))
    norm_gain = jnp.clip(1.0 + 0.15 * jax.random.normal(keys[4], (D,), jnp.float32), 0.25, 1.75).astype(jnp.bfloat16)
    weight_in = bell_draw(keys[5], (H, D), D ** -0.5, 0.21875, ((0, 16),))
    bias_in = bell_draw(keys[6], (H,), 0.5, 3.0, ((0, 16),))
    weight_out = bell_draw(keys[7], (H, D), H ** -0.5, 0.109375, ((0, 16),))
    bias_out = bell_draw(keys[8], (D,), 0.5, 3.0)
    tool_embeds = draw_tool_embeds(jax.random.fold_in(keys[11], 71), 0)
    positive = place_ends(jax.random.randint(keys[10], (CHAINS,), 0, TB), jax.random.fold_in(keys[10], 1), 0, TB - 1).astype(jnp.int32)
    return {"queries": queries, "first_owner": first_owner, "first_row": first_row, "tool_table": tool_table, "norm_gain": norm_gain, "weight_in": weight_in, "bias_in": bias_in, "weight_out": weight_out, "bias_out": bias_out, "tool_embeds": tool_embeds, "positive": positive}


def layer_normed(combined, norm_gain):
    row_mean = lax.optimization_barrier(jnp.mean(combined, axis=1, keepdims=True))
    centred = combined - row_mean
    spread = lax.optimization_barrier(jnp.mean(centred * centred, axis=1, keepdims=True))
    return (centred * lax.rsqrt(spread + 1e-05) * norm_gain.astype(jnp.float32)[None, :]).astype(jnp.bfloat16)

def reference(queries, first_owner, first_row, tool_table, norm_gain, weight_in, bias_in, weight_out, bias_out, tool_embeds, positive):
    picked = (first_owner[:, 0] * ROWS_OWN + first_row).astype(jnp.int32)
    first_rows = jnp.take(tool_table, picked, axis=0)
    combined = queries.astype(jnp.float32) + first_rows.astype(jnp.float32)
    block_count = CHAINS // CH_DEV
    tool_ids = jnp.arange(TB, dtype=jnp.int32)

    def one_block(running, inputs):
        block_comb, block_pos = inputs
        normed = layer_normed(block_comb, norm_gain)
        preact = jnp.dot(normed, weight_in.T, preferred_element_type=jnp.float32) + bias_in.astype(jnp.float32)[None, :]
        activated = jax.nn.gelu(preact, approximate=True).astype(jnp.bfloat16)
        branch_sum = jnp.dot(activated, weight_out, preferred_element_type=jnp.float32)
        updated = (block_comb + branch_sum + bias_out.astype(jnp.float32)[None, :]).astype(jnp.bfloat16)
        scores = jnp.dot(updated, tool_embeds.T, preferred_element_type=jnp.float32)
        row_max = lax.optimization_barrier(jnp.max(scores, axis=1, keepdims=True))
        log_total = row_max + jnp.log(lax.optimization_barrier(jnp.sum(jnp.exp(scores - row_max), axis=1, keepdims=True)))
        is_positive = (tool_ids[None, :] == block_pos[:, None]).astype(jnp.float32)
        chain_loss = log_total[:, 0] - lax.optimization_barrier(jnp.sum(scores * is_positive, axis=1))
        weights_grad = (jnp.exp(scores - log_total) - is_positive).astype(jnp.bfloat16)
        query_grad = jnp.dot(weights_grad, tool_embeds, preferred_element_type=jnp.float32)
        running = running + jnp.dot(weights_grad.T, updated, preferred_element_type=jnp.float32)
        return (running, (updated, chain_loss, query_grad))
    running, outputs = lax.scan(one_block, jnp.zeros((TB, D), jnp.float32), (combined.reshape(block_count, CH_DEV, D), positive.reshape(block_count, CH_DEV)))
    updated, chain_loss, query_grad = outputs
    tool_grad = running * (TB / CHAINS) ** 0.5
    return (updated.reshape(CHAINS, D), chain_loss.reshape(CHAINS), query_grad.reshape(CHAINS, D), tool_grad)
```

```python
import functools

import jax
import jax.numpy as jnp
from jax import lax
from jax.experimental import pallas as pl
from jax.experimental.pallas import tpu as pltpu
from jax.sharding import PartitionSpec as P

F32 = jnp.float32
BF16 = jnp.bfloat16
VMEM_BYTES = 48 * 1024 * 1024


def flipped(block, axis, mask):
    return lax.ppermute(block, axis, [(i, i ^ mask) for i in range(lax.axis_size(axis))])


def kernel_call(body, out_shape, *args, smem=()):
    return pl.pallas_call(
        body,
        out_shape=out_shape,
        in_specs=[
            pl.BlockSpec(memory_space=pltpu.SMEM if i in smem else pltpu.VMEM) for i in range(len(args))
        ],
        out_specs=jax.tree.map(lambda _: pl.BlockSpec(memory_space=pltpu.VMEM), out_shape),
        compiler_params=pltpu.CompilerParams(vmem_limit_bytes=VMEM_BYTES),
    )(*args)


def iota(shape, dimension):
    return lax.broadcasted_iota(jnp.int32, shape, dimension)


def slots_of(owner, groups, capacity):
    chains = owner.shape[0]
    marks = (owner == iota((chains, groups), 1)).astype(F32)
    before = (iota((chains, chains), 1) < iota((chains, chains), 0)).astype(BF16)
    counts = jnp.dot(before, marks.astype(BF16), preferred_element_type=F32)
    rank = jnp.sum(counts * marks, axis=1, keepdims=True)
    return marks, rank, owner.astype(F32) * capacity + rank


def request_body(groups, capacity, owner_ref, row_ref, bias_ref, message_ref):
    owner = owner_ref[...]
    chains = owner.shape[0]
    bias_count = bias_ref.shape[1]
    marks, rank, _ = slots_of(owner, groups, capacity)
    ranked = (rank.astype(jnp.int32) == iota((chains, capacity), 1)).astype(F32) * row_ref[...].astype(F32)
    request = lax.dot_general(
        marks.astype(BF16), ranked.astype(BF16), (((0,), (0,)), ((), ())), preferred_element_type=F32
    )
    message_ref[...] = jnp.zeros_like(message_ref)
    message_ref[:, :bias_count] = jnp.broadcast_to(bias_ref[...].astype(F32), (groups, bias_count))
    message_ref[:, bias_count : bias_count + capacity] = request


def serve_body(capacity, bias_count, message_ref, table_ref, rows_ref):
    groups = message_ref.shape[0]
    slots, held = groups * capacity, table_ref.shape[0]
    wanted = message_ref[:, bias_count : bias_count + capacity].astype(BF16)
    spread = (iota((slots, groups), 0) // capacity == iota((slots, groups), 1)).astype(BF16)
    by_rank = jnp.dot(spread, wanted, preferred_element_type=F32)
    mine = (iota((slots, capacity), 0) % capacity == iota((slots, capacity), 1)).astype(F32)
    row = jnp.sum(by_rank * mine, axis=1, keepdims=True).astype(jnp.int32)
    pick = (row == iota((slots, held), 1)).astype(BF16)
    rows_ref[...] = jnp.dot(pick, table_ref[...], preferred_element_type=F32).astype(BF16)


def select_body(groups, capacity, owner_ref, fetched_ref, rows_ref):
    owner = owner_ref[...]
    _, _, slot = slots_of(owner, groups, capacity)
    pick = (slot.astype(jnp.int32) == iota((owner.shape[0], groups * capacity), 1)).astype(BF16)
    rows_ref[...] = jnp.dot(pick, fetched_ref[...], preferred_element_type=F32).astype(BF16)


def norm_body(queries_ref, queries2_ref, rows_ref, rows2_ref, gain_ref, combined_ref, normed_ref):
    chains = queries_ref.shape[0]
    gain = gain_ref[...].astype(F32)
    for at, (q_ref, r_ref) in enumerate(((queries_ref, rows_ref), (queries2_ref, rows2_ref))):
        combined = q_ref[...].astype(F32) + r_ref[...].astype(F32)
        centred = combined - jnp.mean(combined, axis=1, keepdims=True)
        spread = jnp.mean(centred * centred, axis=1, keepdims=True)
        combined_ref[at * chains : (at + 1) * chains, :] = combined
        normed_ref[at * chains : (at + 1) * chains, :] = (centred * lax.rsqrt(spread + 1e-05) * gain).astype(BF16)


def gelu(u):
    return 0.5 * u * (1.0 + jnp.tanh(0.7978845608028654 * (u + 0.044715 * (u * u * u))))


def hidden_body(plan, me_ref, normed_ref, message_ref, *refs):
    pieces, total_ref = refs[:-1], refs[-1]
    normed = normed_ref[...]
    me = me_ref[0]
    total = None
    for place, (in_at, in_row), (out_at, out_row), units in plan:
        preact = lax.dot_general(
            normed,
            pieces[in_at][in_row : in_row + units, :],
            (((1,), (1,)), ((), ())),
            preferred_element_type=F32,
        )
        bias = message_ref[pl.ds(me ^ place, 1), :][:, :units]
        activated = gelu(preact + bias).astype(BF16)
        term = jnp.dot(activated, pieces[out_at][out_row : out_row + units, :], preferred_element_type=F32)
        total = term if total is None else total + term
    total_ref[...] = total


def score_body(
    own_blocks,
    combined_ref,
    partial_ref,
    partial2_ref,
    bias_ref,
    tools_ref,
    columns_ref,
    positive_ref,
    updated_ref,
    loss_ref,
    weights_ref,
    *grad_refs,
):
    chains = updated_ref.shape[0]
    block_rows = tools_ref.shape[0] // own_blocks[1]
    both = combined_ref.shape[0]
    branch = partial_ref[...] + jnp.concatenate([partial2_ref[chains:, :], partial2_ref[:chains, :]], axis=0)
    updated = (combined_ref[...] + branch + bias_ref[...].astype(F32)).astype(BF16)
    updated_ref[...] = updated[:chains, :]
    scores = lax.dot_general(updated, tools_ref[...], (((1,), (1,)), ((), ())), preferred_element_type=F32)
    row_max = jnp.max(scores, axis=1, keepdims=True)
    log_total = row_max + jnp.log(jnp.sum(jnp.exp(scores - row_max), axis=1, keepdims=True))
    is_positive = (columns_ref[...] == positive_ref[...]).astype(F32)
    loss_ref[...] = (log_total - jnp.sum(scores * is_positive, axis=1, keepdims=True))[:chains, :]
    weights = (jnp.exp(scores - log_total) - is_positive).astype(BF16)
    weights_ref[...] = weights[:chains, :]
    for grad_ref, block in zip(grad_refs, own_blocks[0]):
        grad_ref[...] = lax.dot_general(
            weights[:, block * block_rows : (block + 1) * block_rows],
            updated,
            (((0,), (0,)), ((), ())),
            preferred_element_type=F32,
        ).astype(BF16)


def weight_pieces(own, units, groups):
    arrays, plan = [], []

    def whole(place, shard):
        arrays.append(shard)
        plan.append((place, (len(arrays) - 1, 0), (len(arrays) - 1, units), units))

    def halves(place, in_half, out_half):
        arrays.extend((in_half, out_half))
        plan.append((place, (len(arrays) - 2, 0), (len(arrays) - 1, 0), units))

    levels = range(0, groups, 4)
    column = {0: own}
    for level in levels:
        if level:
            column[level] = flipped(own, "mp", level)
    diagonal = flipped(own, "mp", 3)
    for level in levels:
        shard = column[level]
        by_x, by_y = flipped(shard, "mp", 1), flipped(shard, "mp", 2)
        whole(level, shard)
        whole(level ^ 1, by_x)
        whole(level ^ 2, by_y)
        if level == 0:
            whole(level ^ 3, diagonal)
        elif level == 4:
            whole(level ^ 3, flipped(diagonal, "mp", 4))
        else:
            halves(level ^ 3, flipped(by_y[:units], "mp", 1), flipped(by_x[units:], "mp", 2))
    return arrays, tuple(plan)


def local(
    queries,
    first_owner,
    first_row,
    tool_table,
    norm_gain,
    weight_in,
    bias_in,
    weight_out,
    bias_out,
    tool_embeds,
    positive,
):
    chains, features = queries.shape
    groups, cycle = lax.axis_size("mp"), lax.axis_size("dp")
    me, core = lax.axis_index("mp"), lax.axis_index("dp")
    capacity = 2 * chains // groups
    slots = groups * capacity
    units = weight_in.shape[0] // 2
    block_rows = tool_embeds.shape[0]
    half = core % 2

    own = jnp.concatenate(
        [
            lax.dynamic_slice_in_dim(weight_in, half * units, units, 0),
            lax.dynamic_slice_in_dim(weight_out, half * units, units, 0),
        ],
        axis=0,
    )
    own_bias = lax.dynamic_slice_in_dim(bias_in, half * units, units, 0)
    arrays, plan = weight_pieces(own, units, groups)

    width = -(-(units + capacity) // 128) * 128
    message = kernel_call(
        functools.partial(request_body, groups, capacity),
        jax.ShapeDtypeStruct((groups, width), F32),
        first_owner,
        first_row[:, None],
        own_bias[None, :],
    )
    asked = lax.all_to_all(message, "mp", split_axis=0, concat_axis=0, tiled=True)
    served = kernel_call(
        functools.partial(serve_body, capacity, units),
        jax.ShapeDtypeStruct((slots, features), BF16),
        asked,
        tool_table,
    )
    fetched = lax.all_to_all(served, "mp", split_axis=0, concat_axis=0, tiled=True)
    first_rows = kernel_call(
        functools.partial(select_body, groups, capacity),
        jax.ShapeDtypeStruct((chains, features), BF16),
        first_owner,
        fetched,
    )
    combined, normed = kernel_call(
        norm_body,
        (
            jax.ShapeDtypeStruct((2 * chains, features), F32),
            jax.ShapeDtypeStruct((2 * chains, features), BF16),
        ),
        queries,
        flipped(queries, "dp", 1),
        first_rows,
        flipped(first_rows, "dp", 1),
        norm_gain[None, :],
    )
    partial = kernel_call(
        functools.partial(hidden_body, plan),
        jax.ShapeDtypeStruct((2 * chains, features), F32),
        me[None],
        normed,
        asked,
        *arrays,
        smem=(0,),
    )

    tools = jnp.concatenate([tool_embeds] + [flipped(tool_embeds, "dp", j) for j in range(1, cycle)], axis=0)
    columns = jnp.concatenate(
        [(core ^ j) * block_rows + jnp.arange(block_rows, dtype=jnp.int32) for j in range(cycle)]
    )
    positives = jnp.concatenate([positive, flipped(positive, "dp", 1)])
    own_blocks = tuple(range(0, cycle, 2))
    updated, loss, weights, *grads = kernel_call(
        functools.partial(score_body, (own_blocks, cycle)),
        (
            jax.ShapeDtypeStruct((chains, features), BF16),
            jax.ShapeDtypeStruct((chains, 1), F32),
            jax.ShapeDtypeStruct((chains, block_rows * cycle), BF16),
        )
        + tuple(jax.ShapeDtypeStruct((block_rows, features), BF16) for _ in own_blocks),
        combined,
        partial,
        flipped(partial, "dp", 1),
        bias_out[None, :],
        tools,
        columns[None, :],
        positives[:, None],
    )
    query_grad = jnp.dot(weights, tools, preferred_element_type=F32)

    grad = grads[0].astype(F32)
    for block, term in zip(own_blocks[1:], grads[1:]):
        grad = grad + flipped(term, "dp", block).astype(F32)
    mask = 1
    while mask < groups:
        rounded = grad.astype(BF16)
        grad = rounded.astype(F32) + flipped(rounded, "mp", mask).astype(F32)
        mask *= 2
    grad_scale = (block_rows * cycle / (chains * groups * cycle)) ** 0.5
    return updated, loss[:, 0], query_grad, grad * grad_scale


def solution(mesh):
    in_specs = (
        P(("dp", "mp"), None),
        P(("dp", "mp"), None),
        P(("dp", "mp")),
        P("mp", None),
        P(),
        P("mp", None),
        P("mp"),
        P("mp", None),
        P(),
        P("dp", None),
        P(("dp", "mp")),
    )
    out_specs = (P(("dp", "mp"), None), P(("dp", "mp")), P(("dp", "mp"), None), P("dp", None))
    return jax.shard_map(local, mesh=mesh, in_specs=in_specs, out_specs=out_specs, check_vma=False)
```

```python
import functools

import jax
import jax.numpy as jnp
from jax import lax
from jax.experimental import pallas as pl
from jax.experimental.pallas import tpu as pltpu
from jax.sharding import PartitionSpec as P

F32 = jnp.float32
BF16 = jnp.bfloat16
DIGIT = 256
TILE_ROWS = 16
SMALL_VMEM = 6 * 1024 * 1024
LARGE_VMEM = 14 * 1024 * 1024


def flipped(block, axis, mask):
    return lax.ppermute(block, axis, [(i, i ^ mask) for i in range(lax.axis_size(axis))])


def moved(block, *moves):
    cycle, groups = lax.axis_size("dp"), lax.axis_size("mp")
    route = [
        ((d ^ to ^ source) * groups + (i ^ mask), d * groups + i)
        for to, source, mask in moves
        for d in range(to, cycle, 2)
        for i in range(groups)
    ]
    return lax.ppermute(block, ("dp", "mp"), route)


def after(value, *others):
    return lax.optimization_barrier((value, *others))[0]


def kernel_call(body, out_shape, *args, in_place=(), scratch=(), vmem=SMALL_VMEM):
    return pl.pallas_call(
        body,
        out_shape=out_shape,
        in_specs=[
            pl.BlockSpec(memory_space=pltpu.HBM if i in in_place else pltpu.VMEM) for i in range(len(args))
        ],
        out_specs=jax.tree.map(lambda _: pl.BlockSpec(memory_space=pltpu.VMEM), out_shape),
        scratch_shapes=scratch,
        compiler_params=pltpu.CompilerParams(vmem_limit_bytes=vmem),
    )(*args)


def iota(shape, dimension):
    return lax.broadcasted_iota(jnp.int32, shape, dimension)


def slots_of(owner, groups):
    chains = owner.shape[1]
    marks = (owner == iota((groups, chains), 0)).astype(F32)
    before = (iota((chains, chains), 0) < iota((chains, chains), 1)).astype(BF16)
    counts = jnp.dot(marks.astype(BF16), before, preferred_element_type=F32)
    return marks, jnp.sum(counts * marks, axis=0, keepdims=True)


def request_body(capacity, owner_ref, row_ref, bias_ref, message_ref):
    groups, _, width = message_ref.shape
    bias_count = bias_ref.shape[1]
    marks, rank = slots_of(owner_ref[...], groups)
    ranked = (rank.astype(jnp.int32) == iota((capacity, rank.shape[1]), 0)).astype(F32) * row_ref[...].astype(F32)
    request = lax.dot_general(
        marks.astype(BF16), ranked.astype(BF16), (((1,), (1,)), ((), ())), preferred_element_type=F32
    )
    bias = jnp.broadcast_to(bias_ref[...].astype(F32), (groups, bias_count))
    rest = jnp.zeros((groups, width - bias_count - capacity), F32)
    message_ref[...] = jnp.concatenate([bias, request, rest], axis=1).reshape(message_ref.shape)


def serve_body(capacity, bias_count, message_ref, table_ref, rows_ref):
    groups = message_ref.shape[0]
    slots, held = groups * capacity, table_ref.shape[0]
    message = message_ref[...].reshape(groups, message_ref.shape[2])
    wanted = message[:, bias_count : bias_count + capacity].astype(BF16)
    spread = (iota((slots, groups), 0) // capacity == iota((slots, groups), 1)).astype(BF16)
    by_rank = jnp.dot(spread, wanted, preferred_element_type=F32)
    mine = (iota((slots, capacity), 0) % capacity == iota((slots, capacity), 1)).astype(F32)
    row = jnp.sum(by_rank * mine, axis=1, keepdims=True).astype(jnp.int32)
    pick = (row == iota((slots, held), 1)).astype(BF16)
    rows_ref[...] = jnp.dot(pick, table_ref[...], preferred_element_type=F32).astype(BF16)


def pack_body(capacity, groups, owner_ref, positive_ref, gain_ref, bias_ref, queries_ref, packed_ref):
    chains, features = queries_ref.shape
    owner, positive = owner_ref[...], positive_ref[...]
    _, rank = slots_of(owner, groups)
    slot = owner * capacity + rank.astype(jnp.int32)
    small = jnp.concatenate([slot, positive // DIGIT, positive % DIGIT], axis=0).astype(F32)
    small = jnp.concatenate([small, jnp.zeros((3, features - chains), F32)], axis=1)
    wide = jnp.concatenate([gain_ref[...], bias_ref[...]], axis=0).astype(F32)
    rest = jnp.zeros((TILE_ROWS - 5, features), F32)
    packed_ref[:chains, :] = queries_ref[...]
    packed_ref[chains:, :] = jnp.concatenate([small, wide, rest], axis=0).astype(BF16)


def select_body(packed_ref, fetched_ref, shifted_ref, normed_ref, positive_ref):
    slots = fetched_ref.shape[0]
    chains = shifted_ref.shape[0]
    extra = packed_ref[chains:, :].astype(F32)
    digits = extra[:3, :chains].astype(jnp.int32)
    positive_ref[...] = digits[1:2, :] * DIGIT + digits[2:3, :]
    pick = (digits[0:1, :] == iota((slots, chains), 0)).astype(F32).T.astype(BF16)
    rows = jnp.dot(pick, fetched_ref[...], preferred_element_type=F32)
    combined = packed_ref[:chains, :].astype(F32) + rows
    centred = combined - jnp.mean(combined, axis=1, keepdims=True)
    spread = jnp.mean(centred * centred, axis=1, keepdims=True)
    normed_ref[...] = (centred * lax.rsqrt(spread + 1e-05) * extra[3:4, :]).astype(BF16)
    shifted_ref[...] = combined + extra[4:5, :]


def gelu(u):
    return 0.5 * u * (1.0 + jnp.tanh(0.7978845608028654 * (u + 0.044715 * (u * u * u))))


def hidden_body(plan, normed_ref, normed2_ref, message_ref, *refs):
    shards, (total_ref, total2_ref, held, sems) = refs[:-4], refs[-4:]
    chains, units = total_ref.shape[0], held.shape[1] // 2
    me, first_core = lax.axis_index("mp"), lax.axis_index("dp") % 2 == 0

    def copy(at, p):
        return pltpu.make_async_copy(shards[at], held.at[p], sems.at[p])

    for p, (_, at, _, other_at) in enumerate(plan):
        if at == other_at:
            copy(at, p).start()
        else:
            pl.when(first_core)(copy(at, p).start)
            pl.when(jnp.logical_not(first_core))(copy(other_at, p).start)
    normed = jnp.concatenate([normed_ref[...], normed2_ref[...]], axis=0)
    total = None
    for p, (mask, at, other_mask, _) in enumerate(plan):
        copy(at, p).wait()
        preact = lax.dot_general(
            normed, held[p, :units, :], (((1,), (1,)), ((), ())), preferred_element_type=F32
        )
        bias = message_ref[pl.ds(me ^ jnp.where(first_core, mask, other_mask), 1)]
        activated = gelu(preact + bias.reshape(1, bias.shape[2])[:, :units]).astype(BF16)
        term = jnp.dot(activated, held[p, units:, :], preferred_element_type=F32)
        total = term if total is None else total + term
    total_ref[...] = total[:chains, :]
    total2_ref[...] = total[chains:, :]


def add_body(total_ref, received_ref, sum_ref):
    sum_ref[...] = (total_ref[...] + received_ref[...]).astype(sum_ref.dtype)


def score_body(
    blocks,
    shifted_ref,
    total_ref,
    received_ref,
    other_ref,
    positive_ref,
    *refs,
):
    tools = [ref[...] for ref in refs[:blocks]]
    updated_ref, loss_ref, weights_ref, *grad_refs = refs[blocks:]
    block_rows = tools[0].shape[0]
    branch = total_ref[...] + received_ref[...] + other_ref[...].astype(F32)
    updated = (shifted_ref[...] + branch).astype(BF16)
    updated_ref[...] = updated
    scores = jnp.concatenate(
        [
            lax.dot_general(updated, t, (((1,), (1,)), ((), ())), preferred_element_type=F32)
            for t in tools
        ],
        axis=1,
    )
    tool = iota((scores.shape[1], scores.shape[0]), 0)
    column = ((tool // block_rows) ^ lax.axis_index("dp")) * block_rows + tool % block_rows
    is_positive = (column == positive_ref[...]).astype(F32).T
    row_max = jnp.max(scores, axis=1, keepdims=True)
    log_total = row_max + jnp.log(jnp.sum(jnp.exp(scores - row_max), axis=1, keepdims=True))
    loss_ref[...] = log_total - jnp.sum(scores * is_positive, axis=1, keepdims=True)
    weights = (jnp.exp(scores - log_total) - is_positive).astype(BF16)
    weights_ref[...] = weights
    for block, grad_ref in enumerate(grad_refs):
        grad_ref[...] = lax.dot_general(
            weights[:, block * block_rows : (block + 1) * block_rows],
            updated,
            (((0,), (0,)), ((), ())),
            preferred_element_type=F32,
        ).astype(BF16)


def query_grad_body(weights_ref, *refs):
    tool_refs, grad_ref = refs[:-1], refs[-1]
    block_rows = tool_refs[0].shape[0]
    grad_ref[...] = sum(
        jnp.dot(
            weights_ref[:, j * block_rows : (j + 1) * block_rows], ref[...], preferred_element_type=F32
        )
        for j, ref in enumerate(tool_refs)
    )


def weight_pieces(own, own_later, groups, hold):
    near = moved(own, (0, 0, 1), (1, 1, 8))
    near_y = moved(own_later, (0, 0, 2))
    near_both = moved(own_later, (0, 0, 3))
    near, near_y, near_both = hold(near, near_y, near_both)
    far_x, far_y, far_both = (moved(near, (1, 1, mask)) for mask in (1, 2, 3))
    pieces = [(0, own, 8, near), (1, near, 9, far_x), (2, near_y, 10, far_y), (3, near_both, 11, far_both)]
    for level in range(16, groups, 16):
        base = moved(own, (0, 0, level), (1, 1, level ^ 8))
        by_x, by_y = (moved(base, (0, 0, bit), (1, 1, bit)) for bit in (1, 2))
        both = moved(by_x, (0, 0, 2), (1, 1, 2))
        pieces += [(level ^ m, s, level ^ 8 ^ m, s) for m, s in enumerate((base, by_x, by_y, both))]
    return pieces


def local(
    queries,
    first_owner,
    first_row,
    tool_table,
    norm_gain,
    weight_in,
    bias_in,
    weight_out,
    bias_out,
    tool_embeds,
    positive,
):
    chains, features = queries.shape
    groups, cycle = lax.axis_size("mp"), lax.axis_size("dp")
    capacity = 2 * chains // groups
    slots = groups * capacity
    units = weight_in.shape[0]
    block_rows = tool_embeds.shape[0]
    tool_count = block_rows * cycle

    def whole(shape, dtype):
        return jax.ShapeDtypeStruct(shape, dtype)

    owner_row = first_owner.reshape(1, chains)
    width = -(-(units + capacity) // 128) * 128
    message = kernel_call(
        functools.partial(request_body, capacity),
        whole((groups, 1, width), F32),
        owner_row,
        first_row.reshape(1, chains),
        bias_in.reshape(1, units),
    )
    asked = lax.all_to_all(message, "mp", split_axis=0, concat_axis=0, tiled=True)
    packed = kernel_call(
        functools.partial(pack_body, capacity, groups),
        whole((chains + TILE_ROWS, features), BF16),
        after(owner_row, message),
        positive.reshape(1, chains),
        norm_gain.reshape(1, features),
        bias_out.reshape(1, features),
        queries,
    )
    served = kernel_call(
        functools.partial(serve_body, capacity, units),
        whole((slots, features), BF16),
        after(asked, packed),
        tool_table,
    )
    own = jnp.concatenate([weight_in, weight_out], axis=0)
    own_later = after(own, message)
    held = []

    def hold(*early):
        early_and_served = lax.optimization_barrier((*early, served))
        held.append(early_and_served[-1])
        return early_and_served[:-1]

    pieces = weight_pieces(own, own_later, groups, hold)
    fetched = lax.all_to_all(held[0], "mp", split_axis=0, concat_axis=0, tiled=True)
    shards = []
    for piece in pieces:
        for shard in (piece[1], piece[3]):
            if all(shard is not s for s in shards):
                shards.append(shard)
    index_of = {id(s): i for i, s in enumerate(shards)}
    plan = tuple((mask, index_of[id(s)], other, index_of[id(t)]) for mask, s, other, t in pieces)

    shifted, normed, positive_row = kernel_call(
        select_body,
        (whole((chains, features), F32), whole((chains, features), BF16), whole((1, chains), jnp.int32)),
        packed,
        fetched,
    )

    def hidden(own_rows):
        return kernel_call(
            functools.partial(hidden_body, plan),
            (whole((chains, features), F32),) * 2,
            own_rows,
            flipped(own_rows, "dp", 1),
            asked,
            *shards,
            in_place=range(3, 3 + len(shards)),
            scratch=(pltpu.VMEM((len(plan), 2 * units, features), BF16), pltpu.SemaphoreType.DMA((len(plan),))),
            vmem=LARGE_VMEM,
        )

    total, total_for = hidden(normed)
    neighbour, neighbour_for = hidden(after(flipped(normed, "mp", 4), total))
    neighbour_sum = kernel_call(
        add_body, whole((chains, features), BF16), neighbour, flipped(neighbour_for, "dp", 1)
    )
    late_tools = after(tool_embeds, total)
    tools = [tool_embeds] + [flipped(late_tools, "dp", j) for j in range(1, cycle)]
    updated, loss, weights, *grads = kernel_call(
        functools.partial(score_body, cycle),
        (
            whole((chains, features), BF16),
            whole((chains, 1), F32),
            whole((chains, tool_count), BF16),
            *(whole((block_rows, features), BF16) for _ in range(cycle)),
        ),
        shifted,
        total,
        flipped(total_for, "dp", 1),
        flipped(neighbour_sum, "mp", 4),
        positive_row,
        *tools,
    )
    query_grad = kernel_call(query_grad_body, whole((chains, features), F32), weights, *tools)

    grad = grads[0].astype(F32)
    for block in range(1, cycle):
        grad = grad + flipped(grads[block], "dp", block).astype(F32)
    bits = [1 << b for b in range((groups - 1).bit_length())]
    turned = bits[len(bits) // 2 :] + bits[: len(bits) // 2]
    for bit, other_bit in zip(bits, turned):
        rounded = grad.astype(BF16)
        grad = rounded.astype(F32) + moved(rounded, (0, 0, bit), (1, 1, other_bit)).astype(F32)
    grad_scale = (tool_count / (chains * groups * cycle)) ** 0.5
    return updated, loss[:, 0], query_grad, grad * grad_scale


def solution(mesh):
    in_specs = (
        P(("dp", "mp"), None),
        P(("dp", "mp"), None),
        P(("dp", "mp")),
        P("mp", None),
        P(),
        P("mp", None),
        P("mp"),
        P("mp", None),
        P(),
        P("dp", None),
        P(("dp", "mp")),
    )
    out_specs = (P(("dp", "mp"), None), P(("dp", "mp")), P(("dp", "mp"), None), P("dp", None))
    return jax.shard_map(local, mesh=mesh, in_specs=in_specs, out_specs=out_specs, check_vma=False)
```

```python
import functools

import jax
import jax.numpy as jnp
from jax import lax
from jax.experimental import pallas as pl
from jax.experimental.pallas import tpu as pltpu
from jax.sharding import PartitionSpec as P

F32 = jnp.float32
BF16 = jnp.bfloat16
DIGIT = 256
TILE_ROWS = 16
SMALL_VMEM = 6 * 1024 * 1024
LARGE_VMEM = 14 * 1024 * 1024


def flipped(block, axis, mask):
    return lax.ppermute(block, axis, [(i, i ^ mask) for i in range(lax.axis_size(axis))])


def moved(block, *moves):
    cycle, groups = lax.axis_size("dp"), lax.axis_size("mp")
    route = [
        ((d ^ to ^ source) * groups + (i ^ mask), d * groups + i)
        for to, source, mask in moves
        for d in range(to, cycle, 2)
        for i in range(groups)
    ]
    return lax.ppermute(block, ("dp", "mp"), route)


def after(value, *others):
    return lax.optimization_barrier((value, *others))[0]


def kernel_call(body, out_shape, *args, in_place=(), scratch=(), vmem=SMALL_VMEM):
    return pl.pallas_call(
        body,
        out_shape=out_shape,
        in_specs=[
            pl.BlockSpec(memory_space=pltpu.HBM if i in in_place else pltpu.VMEM) for i in range(len(args))
        ],
        out_specs=jax.tree.map(lambda _: pl.BlockSpec(memory_space=pltpu.VMEM), out_shape),
        scratch_shapes=scratch,
        compiler_params=pltpu.CompilerParams(vmem_limit_bytes=vmem),
    )(*args)


def iota(shape, dimension):
    return lax.broadcasted_iota(jnp.int32, shape, dimension)


def slots_of(owner, groups):
    chains = owner.shape[1]
    marks = (owner == iota((groups, chains), 0)).astype(F32)
    before = (iota((chains, chains), 0) < iota((chains, chains), 1)).astype(BF16)
    counts = jnp.dot(marks.astype(BF16), before, preferred_element_type=F32)
    return marks, jnp.sum(counts * marks, axis=0, keepdims=True)


def request_body(capacity, owner_ref, row_ref, bias_ref, message_ref):
    groups, _, width = message_ref.shape
    bias_count = bias_ref.shape[1]
    marks, rank = slots_of(owner_ref[...], groups)
    ranked = (rank.astype(jnp.int32) == iota((capacity, rank.shape[1]), 0)).astype(F32) * row_ref[...].astype(F32)
    request = lax.dot_general(
        marks.astype(BF16), ranked.astype(BF16), (((1,), (1,)), ((), ())), preferred_element_type=F32
    )
    bias = jnp.broadcast_to(bias_ref[...].astype(F32), (groups, bias_count))
    rest = jnp.zeros((groups, width - bias_count - capacity), F32)
    message_ref[...] = jnp.concatenate([bias, request, rest], axis=1).reshape(message_ref.shape)


def serve_body(capacity, bias_count, message_ref, table_ref, rows_ref):
    groups = message_ref.shape[0]
    slots, held = groups * capacity, table_ref.shape[0]
    message = message_ref[...].reshape(groups, message_ref.shape[2])
    wanted = message[:, bias_count : bias_count + capacity].astype(BF16)
    spread = (iota((slots, groups), 0) // capacity == iota((slots, groups), 1)).astype(BF16)
    by_rank = jnp.dot(spread, wanted, preferred_element_type=F32)
    mine = (iota((slots, capacity), 0) % capacity == iota((slots, capacity), 1)).astype(F32)
    row = jnp.sum(by_rank * mine, axis=1, keepdims=True).astype(jnp.int32)
    pick = (row == iota((slots, held), 1)).astype(BF16)
    rows_ref[...] = jnp.dot(pick, table_ref[...], preferred_element_type=F32).astype(BF16)


def pack_body(capacity, groups, owner_ref, positive_ref, gain_ref, bias_ref, queries_ref, packed_ref):
    chains, features = queries_ref.shape
    owner, positive = owner_ref[...], positive_ref[...]
    _, rank = slots_of(owner, groups)
    slot = owner * capacity + rank.astype(jnp.int32)
    small = jnp.concatenate([slot, positive // DIGIT, positive % DIGIT], axis=0).astype(F32)
    small = jnp.concatenate([small, jnp.zeros((3, features - chains), F32)], axis=1)
    wide = jnp.concatenate([gain_ref[...], bias_ref[...]], axis=0).astype(F32)
    rest = jnp.zeros((TILE_ROWS - 5, features), F32)
    packed_ref[:chains, :] = queries_ref[...]
    packed_ref[chains:, :] = jnp.concatenate([small, wide, rest], axis=0).astype(BF16)


def select_body(packed_ref, fetched_ref, shifted_ref, normed_ref, positive_ref):
    slots = fetched_ref.shape[0]
    chains = shifted_ref.shape[0]
    extra = packed_ref[chains:, :].astype(F32)
    digits = extra[:3, :chains].astype(jnp.int32)
    positive_ref[...] = digits[1:2, :] * DIGIT + digits[2:3, :]
    pick = (digits[0:1, :] == iota((slots, chains), 0)).astype(F32).T.astype(BF16)
    rows = jnp.dot(pick, fetched_ref[...], preferred_element_type=F32)
    combined = packed_ref[:chains, :].astype(F32) + rows
    centred = combined - jnp.mean(combined, axis=1, keepdims=True)
    spread = jnp.mean(centred * centred, axis=1, keepdims=True)
    normed_ref[...] = (centred * lax.rsqrt(spread + 1e-05) * extra[3:4, :]).astype(BF16)
    shifted_ref[...] = combined + extra[4:5, :]


def gelu(u):
    return 0.5 * u * (1.0 + jnp.tanh(0.7978845608028654 * (u + 0.044715 * (u * u * u))))


def hidden_body(plan, normed_ref, normed2_ref, message_ref, *refs):
    shards, (total_ref, total2_ref, held_in, held_out, sems) = refs[:-5], refs[-5:]
    chains, units = total_ref.shape[0], held_in.shape[0] // len(plan)
    me, first_core = lax.axis_index("mp"), lax.axis_index("dp") % 2 == 0
    held = (held_in, held_out)

    def copy(at, p, side):
        return pltpu.make_async_copy(
            shards[at].at[pl.ds(side * units, units)], held[side].at[pl.ds(p * units, units)], sems.at[side, p]
        )

    for side in (0, 1):
        for p, (_, at, _, other_at) in enumerate(plan):
            if at == other_at:
                copy(at, p, side).start()
            else:

                @pl.when(first_core)
                def _():
                    copy(at, p, side).start()

                @pl.when(jnp.logical_not(first_core))
                def _():
                    copy(other_at, p, side).start()

    normed = jnp.concatenate([normed_ref[...], normed2_ref[...]], axis=0)
    places = [me ^ jnp.where(first_core, mask, other_mask) for mask, _, other_mask, _ in plan]
    bias = jnp.concatenate(
        [message_ref[pl.ds(place, 1)].reshape(1, message_ref.shape[2])[:, :units] for place in places], axis=1
    )
    for p, (_, at, _, _) in enumerate(plan):
        copy(at, p, 0).wait()
    preact = lax.dot_general(normed, held_in[...], (((1,), (1,)), ((), ())), preferred_element_type=F32)
    activated = gelu(preact + bias).astype(BF16)
    for p, (_, at, _, _) in enumerate(plan):
        copy(at, p, 1).wait()
    total = jnp.dot(activated, held_out[...], preferred_element_type=F32)
    total_ref[...] = total[:chains, :]
    total2_ref[...] = total[chains:, :]


def add_body(total_ref, received_ref, sum_ref):
    sum_ref[...] = (total_ref[...] + received_ref[...]).astype(sum_ref.dtype)


def score_body(
    blocks,
    shifted_ref,
    total_ref,
    received_ref,
    other_ref,
    positive_ref,
    *refs,
):
    tools = [ref[...] for ref in refs[:blocks]]
    updated_ref, loss_ref, weights_ref, *grad_refs = refs[blocks:]
    block_rows = tools[0].shape[0]
    branch = total_ref[...] + received_ref[...] + other_ref[...].astype(F32)
    updated = (shifted_ref[...] + branch).astype(BF16)
    updated_ref[...] = updated
    scores = jnp.concatenate(
        [
            lax.dot_general(updated, t, (((1,), (1,)), ((), ())), preferred_element_type=F32)
            for t in tools
        ],
        axis=1,
    )
    tool = iota((scores.shape[1], scores.shape[0]), 0)
    column = ((tool // block_rows) ^ lax.axis_index("dp")) * block_rows + tool % block_rows
    is_positive = (column == positive_ref[...]).astype(F32).T
    row_max = jnp.max(scores, axis=1, keepdims=True)
    log_total = row_max + jnp.log(jnp.sum(jnp.exp(scores - row_max), axis=1, keepdims=True))
    loss_ref[...] = log_total - jnp.sum(scores * is_positive, axis=1, keepdims=True)
    weights = (jnp.exp(scores - log_total) - is_positive).astype(BF16)
    weights_ref[...] = weights
    for block, grad_ref in enumerate(grad_refs):
        grad_ref[...] = lax.dot_general(
            weights[:, block * block_rows : (block + 1) * block_rows],
            updated,
            (((0,), (0,)), ((), ())),
            preferred_element_type=F32,
        ).astype(BF16)


def query_grad_body(weights_ref, *refs):
    tool_refs, grad_ref = refs[:-1], refs[-1]
    block_rows = tool_refs[0].shape[0]
    grad_ref[...] = sum(
        jnp.dot(
            weights_ref[:, j * block_rows : (j + 1) * block_rows], ref[...], preferred_element_type=F32
        )
        for j, ref in enumerate(tool_refs)
    )


def weight_pieces(own, own_later, groups, hold, asked):
    near = moved(own, (0, 0, 1), (1, 1, 8))
    near_y = moved(own_later, (0, 0, 2))
    first = after(near, asked)
    near, near_y = hold(near, near_y)
    turned = moved(first, (0, 0, 2), (1, 1, 2))
    far_x = moved(first, (1, 1, 1))
    far_both = moved(turned, (1, 1, 1))
    pieces = [(0, own, 8, near), (1, near, 9, far_x), (2, near_y, 10, turned), (3, turned, 11, far_both)]
    for level in range(16, groups, 16):
        base = moved(own, (0, 0, level), (1, 1, level ^ 8))
        by_x, by_y = (moved(base, (0, 0, bit), (1, 1, bit)) for bit in (1, 2))
        both = moved(by_x, (0, 0, 2), (1, 1, 2))
        pieces += [(level ^ m, s, level ^ 8 ^ m, s) for m, s in enumerate((base, by_x, by_y, both))]
    return pieces


def local(
    queries,
    first_owner,
    first_row,
    tool_table,
    norm_gain,
    weight_in,
    bias_in,
    weight_out,
    bias_out,
    tool_embeds,
    positive,
):
    chains, features = queries.shape
    groups, cycle = lax.axis_size("mp"), lax.axis_size("dp")
    capacity = 2 * chains // groups
    slots = groups * capacity
    units = weight_in.shape[0]
    block_rows = tool_embeds.shape[0]
    tool_count = block_rows * cycle

    def whole(shape, dtype):
        return jax.ShapeDtypeStruct(shape, dtype)

    owner_row = first_owner.reshape(1, chains)
    width = -(-(units + capacity) // 128) * 128
    message = kernel_call(
        functools.partial(request_body, capacity),
        whole((groups, 1, width), F32),
        owner_row,
        first_row.reshape(1, chains),
        bias_in.reshape(1, units),
    )
    asked = lax.all_to_all(message, "mp", split_axis=0, concat_axis=0, tiled=True)
    packed = kernel_call(
        functools.partial(pack_body, capacity, groups),
        whole((chains + TILE_ROWS, features), BF16),
        after(owner_row, message),
        positive.reshape(1, chains),
        norm_gain.reshape(1, features),
        bias_out.reshape(1, features),
        queries,
    )
    served = kernel_call(
        functools.partial(serve_body, capacity, units),
        whole((slots, features), BF16),
        after(asked, packed),
        tool_table,
    )
    own = jnp.concatenate([weight_in, weight_out], axis=0)
    own_later = after(own, message)
    held = []

    def hold(*early):
        early_and_served = lax.optimization_barrier((*early, served))
        held.append(early_and_served[-1])
        return early_and_served[:-1]

    pieces = weight_pieces(own, own_later, groups, hold, asked)
    fetched = lax.all_to_all(held[0], "mp", split_axis=0, concat_axis=0, tiled=True)
    shards = []
    for piece in pieces:
        for shard in (piece[1], piece[3]):
            if all(shard is not s for s in shards):
                shards.append(shard)
    index_of = {id(s): i for i, s in enumerate(shards)}
    plan = tuple((mask, index_of[id(s)], other, index_of[id(t)]) for mask, s, other, t in pieces)

    shifted, normed, positive_row = kernel_call(
        select_body,
        (whole((chains, features), F32), whole((chains, features), BF16), whole((1, chains), jnp.int32)),
        packed,
        fetched,
    )

    def hidden(own_rows):
        return kernel_call(
            functools.partial(hidden_body, plan),
            (whole((chains, features), F32),) * 2,
            own_rows,
            flipped(own_rows, "dp", 1),
            asked,
            *shards,
            in_place=range(3, 3 + len(shards)),
            scratch=(
                pltpu.VMEM((len(plan) * units, features), BF16),
                pltpu.VMEM((len(plan) * units, features), BF16),
                pltpu.SemaphoreType.DMA((2, len(plan))),
            ),
            vmem=LARGE_VMEM,
        )

    total, total_for = hidden(normed)
    neighbour, neighbour_for = hidden(after(flipped(normed, "mp", 4), total))
    neighbour_sum = kernel_call(
        add_body, whole((chains, features), BF16), neighbour, flipped(neighbour_for, "dp", 1)
    )
    late_tools = after(tool_embeds, total)
    tools = [tool_embeds] + [flipped(late_tools, "dp", j) for j in range(1, cycle)]
    updated, loss, weights, *grads = kernel_call(
        functools.partial(score_body, cycle),
        (
            whole((chains, features), BF16),
            whole((chains, 1), F32),
            whole((chains, tool_count), BF16),
            *(whole((block_rows, features), BF16) for _ in range(cycle)),
        ),
        shifted,
        total,
        flipped(total_for, "dp", 1),
        flipped(neighbour_sum, "mp", 4),
        positive_row,
        *tools,
    )
    query_grad = kernel_call(query_grad_body, whole((chains, features), F32), weights, *tools)

    grad = grads[0].astype(F32)
    for block in range(1, cycle):
        grad = grad + flipped(grads[block], "dp", block).astype(F32)
    bits = [1 << b for b in range((groups - 1).bit_length())]
    turned = bits[len(bits) // 2 :] + bits[: len(bits) // 2]
    for bit, other_bit in zip(bits, turned):
        rounded = grad.astype(BF16)
        grad = rounded.astype(F32) + moved(rounded, (0, 0, bit), (1, 1, other_bit)).astype(F32)
    grad_scale = (tool_count / (chains * groups * cycle)) ** 0.5
    return updated, loss[:, 0], query_grad, grad * grad_scale


def solution(mesh):
    in_specs = (
        P(("dp", "mp"), None),
        P(("dp", "mp"), None),
        P(("dp", "mp")),
        P("mp", None),
        P(),
        P("mp", None),
        P("mp"),
        P("mp", None),
        P(),
        P("dp", None),
        P(("dp", "mp")),
    )
    out_specs = (P(("dp", "mp"), None), P(("dp", "mp")), P(("dp", "mp"), None), P("dp", None))
    return jax.shard_map(local, mesh=mesh, in_specs=in_specs, out_specs=out_specs, check_vma=False)
```

```python
import functools

import jax
import jax.numpy as jnp
from jax import lax
from jax.experimental import pallas as pl
from jax.experimental.pallas import tpu as pltpu
from jax.sharding import PartitionSpec as P

F32 = jnp.float32
BF16 = jnp.bfloat16
DIGIT = 256
TILE_ROWS = 16
SMALL_VMEM = 6 * 1024 * 1024
LARGE_VMEM = 14 * 1024 * 1024


def flipped(block, axis, mask):
    return lax.ppermute(block, axis, [(i, i ^ mask) for i in range(lax.axis_size(axis))])


def moved(block, *moves):
    cycle, groups = lax.axis_size("dp"), lax.axis_size("mp")
    route = [
        ((d ^ to ^ source) * groups + (i ^ mask), d * groups + i)
        for to, source, mask in moves
        for d in range(to, cycle, 2)
        for i in range(groups)
    ]
    return lax.ppermute(block, ("dp", "mp"), route)


def after(value, *others):
    return lax.optimization_barrier((value, *others))[0]


def kernel_call(body, out_shape, *args, in_place=(), scratch=(), vmem=SMALL_VMEM):
    return pl.pallas_call(
        body,
        out_shape=out_shape,
        in_specs=[
            pl.BlockSpec(memory_space=pltpu.HBM if i in in_place else pltpu.VMEM) for i in range(len(args))
        ],
        out_specs=jax.tree.map(lambda _: pl.BlockSpec(memory_space=pltpu.VMEM), out_shape),
        scratch_shapes=scratch,
        compiler_params=pltpu.CompilerParams(vmem_limit_bytes=vmem),
    )(*args)


def iota(shape, dimension):
    return lax.broadcasted_iota(jnp.int32, shape, dimension)


def slots_of(owner, groups):
    chains = owner.shape[1]
    marks = (owner == iota((groups, chains), 0)).astype(F32)
    before = (iota((chains, chains), 0) < iota((chains, chains), 1)).astype(BF16)
    counts = jnp.dot(marks.astype(BF16), before, preferred_element_type=F32)
    return marks, jnp.sum(counts * marks, axis=0, keepdims=True)


def request_body(capacity, owner_ref, row_ref, bias_ref, message_ref):
    groups, _, width = message_ref.shape
    bias_count = bias_ref.shape[1]
    marks, rank = slots_of(owner_ref[...], groups)
    ranked = (rank.astype(jnp.int32) == iota((capacity, rank.shape[1]), 0)).astype(F32) * row_ref[...].astype(F32)
    request = lax.dot_general(
        marks.astype(BF16), ranked.astype(BF16), (((1,), (1,)), ((), ())), preferred_element_type=F32
    )
    bias = jnp.broadcast_to(bias_ref[...].astype(F32), (groups, bias_count))
    rest = jnp.zeros((groups, width - bias_count - capacity), F32)
    message_ref[...] = jnp.concatenate([bias, request, rest], axis=1).reshape(message_ref.shape)


def serve_body(capacity, bias_count, message_ref, table_ref, rows_ref):
    groups = message_ref.shape[0]
    slots, held = groups * capacity, table_ref.shape[0]
    message = message_ref[...].reshape(groups, message_ref.shape[2])
    wanted = message[:, bias_count : bias_count + capacity].astype(BF16)
    spread = (iota((slots, groups), 0) // capacity == iota((slots, groups), 1)).astype(BF16)
    by_rank = jnp.dot(spread, wanted, preferred_element_type=F32)
    mine = (iota((slots, capacity), 0) % capacity == iota((slots, capacity), 1)).astype(F32)
    row = jnp.sum(by_rank * mine, axis=1, keepdims=True).astype(jnp.int32)
    pick = (row == iota((slots, held), 1)).astype(BF16)
    rows_ref[...] = jnp.dot(pick, table_ref[...], preferred_element_type=F32).astype(BF16)


def pack_body(capacity, groups, owner_ref, positive_ref, gain_ref, bias_ref, queries_ref, packed_ref):
    chains, features = queries_ref.shape
    owner, positive = owner_ref[...], positive_ref[...]
    _, rank = slots_of(owner, groups)
    slot = owner * capacity + rank.astype(jnp.int32)
    small = jnp.concatenate([slot, positive // DIGIT, positive % DIGIT], axis=0).astype(F32)
    small = jnp.concatenate([small, jnp.zeros((3, features - chains), F32)], axis=1)
    wide = jnp.concatenate([gain_ref[...], bias_ref[...]], axis=0).astype(F32)
    rest = jnp.zeros((TILE_ROWS - 5, features), F32)
    packed_ref[:chains, :] = queries_ref[...]
    packed_ref[chains:, :] = jnp.concatenate([small, wide, rest], axis=0).astype(BF16)


def select_body(packed_ref, fetched_ref, shifted_ref, normed_ref, positive_ref):
    slots = fetched_ref.shape[0]
    chains = shifted_ref.shape[0]
    extra = packed_ref[chains:, :].astype(F32)
    digits = extra[:3, :chains].astype(jnp.int32)
    positive_ref[...] = digits[1:2, :] * DIGIT + digits[2:3, :]
    pick = (digits[0:1, :] == iota((slots, chains), 0)).astype(F32).T.astype(BF16)
    rows = jnp.dot(pick, fetched_ref[...], preferred_element_type=F32)
    combined = packed_ref[:chains, :].astype(F32) + rows
    centred = combined - jnp.mean(combined, axis=1, keepdims=True)
    spread = jnp.mean(centred * centred, axis=1, keepdims=True)
    normed_ref[...] = (centred * lax.rsqrt(spread + 1e-05) * extra[3:4, :]).astype(BF16)
    shifted_ref[...] = combined + extra[4:5, :]


def gelu(u):
    return 0.5 * u * (1.0 + jnp.tanh(0.7978845608028654 * (u + 0.044715 * (u * u * u))))


def hidden_body(plan, normed_ref, normed2_ref, message_ref, *refs):
    shards, (total_ref, total2_ref, held_in, held_out, sems) = refs[:-5], refs[-5:]
    chains, units = total_ref.shape[0], held_in.shape[0] // len(plan)
    me, first_core = lax.axis_index("mp"), lax.axis_index("dp") % 2 == 0
    held = (held_in, held_out)

    def copy(at, p, side):
        return pltpu.make_async_copy(
            shards[at].at[pl.ds(side * units, units)], held[side].at[pl.ds(p * units, units)], sems.at[side, p]
        )

    for side in (0, 1):
        for p, (_, at, _, other_at) in enumerate(plan):
            if at == other_at:
                copy(at, p, side).start()
            else:

                @pl.when(first_core)
                def _():
                    copy(at, p, side).start()

                @pl.when(jnp.logical_not(first_core))
                def _():
                    copy(other_at, p, side).start()

    normed = jnp.concatenate([normed_ref[...], normed2_ref[...]], axis=0)
    places = [me ^ jnp.where(first_core, mask, other_mask) for mask, _, other_mask, _ in plan]
    bias = jnp.concatenate(
        [message_ref[pl.ds(place, 1)].reshape(1, message_ref.shape[2])[:, :units] for place in places], axis=1
    )
    for p, (_, at, _, _) in enumerate(plan):
        copy(at, p, 0).wait()
    preact = lax.dot_general(normed, held_in[...], (((1,), (1,)), ((), ())), preferred_element_type=F32)
    activated = gelu(preact + bias).astype(BF16)
    for p, (_, at, _, _) in enumerate(plan):
        copy(at, p, 1).wait()
    total = jnp.dot(activated, held_out[...], preferred_element_type=F32)
    total_ref[...] = total[:chains, :]
    total2_ref[...] = total[chains:, :]


def add_body(total_ref, received_ref, sum_ref):
    sum_ref[...] = (total_ref[...] + received_ref[...]).astype(sum_ref.dtype)


def score_body(
    blocks,
    shifted_ref,
    total_ref,
    received_ref,
    other_ref,
    positive_ref,
    *refs,
):
    tools = [ref[...] for ref in refs[:blocks]]
    updated_ref, loss_ref, weights_ref, *grad_refs = refs[blocks:]
    block_rows = tools[0].shape[0]
    branch = total_ref[...] + received_ref[...] + other_ref[...].astype(F32)
    updated = (shifted_ref[...] + branch).astype(BF16)
    updated_ref[...] = updated
    scores = jnp.concatenate(
        [
            lax.dot_general(updated, t, (((1,), (1,)), ((), ())), preferred_element_type=F32)
            for t in tools
        ],
        axis=1,
    )
    tool = iota((scores.shape[1], scores.shape[0]), 0)
    column = ((tool // block_rows) ^ lax.axis_index("dp")) * block_rows + tool % block_rows
    is_positive = (column == positive_ref[...]).astype(F32).T
    row_max = jnp.max(scores, axis=1, keepdims=True)
    log_total = row_max + jnp.log(jnp.sum(jnp.exp(scores - row_max), axis=1, keepdims=True))
    loss_ref[...] = log_total - jnp.sum(scores * is_positive, axis=1, keepdims=True)
    weights = (jnp.exp(scores - log_total) - is_positive).astype(BF16)
    weights_ref[...] = weights
    for block, grad_ref in enumerate(grad_refs):
        grad_ref[...] = lax.dot_general(
            weights[:, block * block_rows : (block + 1) * block_rows],
            updated,
            (((0,), (0,)), ((), ())),
            preferred_element_type=F32,
        ).astype(BF16)


def query_grad_body(weights_ref, *refs):
    tool_refs, grad_ref = refs[:-1], refs[-1]
    block_rows = tool_refs[0].shape[0]
    grad_ref[...] = sum(
        jnp.dot(
            weights_ref[:, j * block_rows : (j + 1) * block_rows], ref[...], preferred_element_type=F32
        )
        for j, ref in enumerate(tool_refs)
    )


def weight_pieces(own, own_later, groups, hold, asked):
    near = moved(own, (0, 0, 1), (1, 1, 8))
    near_y = moved(own_later, (0, 0, 2))
    first = after(near, asked)
    near, near_y = hold(near, near_y)
    turned = moved(first, (0, 0, 2), (1, 1, 1))
    far_y = moved(first, (1, 1, 2))
    far_both = moved(turned, (1, 1, 2))
    pieces = [(0, own, 8, near), (1, near, 9, turned), (2, near_y, 10, far_y), (3, turned, 11, far_both)]
    for level in range(16, groups, 16):
        base = moved(own, (0, 0, level), (1, 1, level ^ 8))
        by_x, by_y = (moved(base, (0, 0, bit), (1, 1, bit)) for bit in (1, 2))
        both = moved(by_x, (0, 0, 2), (1, 1, 2))
        pieces += [(level ^ m, s, level ^ 8 ^ m, s) for m, s in enumerate((base, by_x, by_y, both))]
    return pieces


def local(
    queries,
    first_owner,
    first_row,
    tool_table,
    norm_gain,
    weight_in,
    bias_in,
    weight_out,
    bias_out,
    tool_embeds,
    positive,
):
    chains, features = queries.shape
    groups, cycle = lax.axis_size("mp"), lax.axis_size("dp")
    capacity = 2 * chains // groups
    slots = groups * capacity
    units = weight_in.shape[0]
    block_rows = tool_embeds.shape[0]
    tool_count = block_rows * cycle

    def whole(shape, dtype):
        return jax.ShapeDtypeStruct(shape, dtype)

    owner_row = first_owner.reshape(1, chains)
    width = -(-(units + capacity) // 128) * 128
    message = kernel_call(
        functools.partial(request_body, capacity),
        whole((groups, 1, width), F32),
        owner_row,
        first_row.reshape(1, chains),
        bias_in.reshape(1, units),
    )
    asked = lax.all_to_all(message, "mp", split_axis=0, concat_axis=0, tiled=True)
    packed = kernel_call(
        functools.partial(pack_body, capacity, groups),
        whole((chains + TILE_ROWS, features), BF16),
        after(owner_row, message),
        positive.reshape(1, chains),
        norm_gain.reshape(1, features),
        bias_out.reshape(1, features),
        queries,
    )
    served = kernel_call(
        functools.partial(serve_body, capacity, units),
        whole((slots, features), BF16),
        after(asked, packed),
        tool_table,
    )
    own = jnp.concatenate([weight_in, weight_out], axis=0)
    own_later = after(own, message)
    held = []

    def hold(*early):
        early_and_served = lax.optimization_barrier((*early, served))
        held.append(early_and_served[-1])
        return early_and_served[:-1]

    pieces = weight_pieces(own, own_later, groups, hold, asked)
    fetched = lax.all_to_all(held[0], "mp", split_axis=0, concat_axis=0, tiled=True)
    shards = []
    for piece in pieces:
        for shard in (piece[1], piece[3]):
            if all(shard is not s for s in shards):
                shards.append(shard)
    index_of = {id(s): i for i, s in enumerate(shards)}
    plan = tuple((mask, index_of[id(s)], other, index_of[id(t)]) for mask, s, other, t in pieces)

    shifted, normed, positive_row = kernel_call(
        select_body,
        (whole((chains, features), F32), whole((chains, features), BF16), whole((1, chains), jnp.int32)),
        packed,
        fetched,
    )

    def hidden(own_rows):
        return kernel_call(
            functools.partial(hidden_body, plan),
            (whole((chains, features), F32),) * 2,
            own_rows,
            flipped(own_rows, "dp", 1),
            asked,
            *shards,
            in_place=range(3, 3 + len(shards)),
            scratch=(
                pltpu.VMEM((len(plan) * units, features), BF16),
                pltpu.VMEM((len(plan) * units, features), BF16),
                pltpu.SemaphoreType.DMA((2, len(plan))),
            ),
            vmem=LARGE_VMEM,
        )

    total, total_for = hidden(normed)
    neighbour, neighbour_for = hidden(after(flipped(normed, "mp", 4), total))
    neighbour_sum = kernel_call(
        add_body, whole((chains, features), BF16), neighbour, flipped(neighbour_for, "dp", 1)
    )
    late_tools = after(tool_embeds, total)
    tools = [tool_embeds] + [flipped(late_tools, "dp", j) for j in range(1, cycle)]
    updated, loss, weights, *grads = kernel_call(
        functools.partial(score_body, cycle),
        (
            whole((chains, features), BF16),
            whole((chains, 1), F32),
            whole((chains, tool_count), BF16),
            *(whole((block_rows, features), BF16) for _ in range(cycle)),
        ),
        shifted,
        total,
        flipped(total_for, "dp", 1),
        flipped(neighbour_sum, "mp", 4),
        positive_row,
        *tools,
    )
    query_grad = kernel_call(query_grad_body, whole((chains, features), F32), weights, *tools)

    grad = grads[0].astype(F32)
    for block in range(1, cycle):
        grad = grad + flipped(grads[block], "dp", block).astype(F32)
    bits = [1 << b for b in range((groups - 1).bit_length())]
    turned = bits[len(bits) // 2 :] + bits[: len(bits) // 2]
    for bit, other_bit in zip(bits, turned):
        rounded = grad.astype(BF16)
        grad = rounded.astype(F32) + moved(rounded, (0, 0, bit), (1, 1, other_bit)).astype(F32)
    grad_scale = (tool_count / (chains * groups * cycle)) ** 0.5
    return updated, loss[:, 0], query_grad, grad * grad_scale


def solution(mesh):
    in_specs = (
        P(("dp", "mp"), None),
        P(("dp", "mp"), None),
        P(("dp", "mp")),
        P("mp", None),
        P(),
        P("mp", None),
        P("mp"),
        P("mp", None),
        P(),
        P("dp", None),
        P(("dp", "mp")),
    )
    out_specs = (P(("dp", "mp"), None), P(("dp", "mp")), P(("dp", "mp"), None), P("dp", None))
    return jax.shard_map(local, mesh=mesh, in_specs=in_specs, out_specs=out_specs, check_vma=False)
```

```python
import functools

import jax
import jax.numpy as jnp
from jax import lax
from jax.experimental import pallas as pl
from jax.experimental.pallas import tpu as pltpu
from jax.sharding import PartitionSpec as P

F32 = jnp.float32
BF16 = jnp.bfloat16
DIGIT = 256
TILE_ROWS = 16
SMALL_VMEM = 6 * 1024 * 1024
LARGE_VMEM = 14 * 1024 * 1024


def flipped(block, axis, mask):
    return lax.ppermute(block, axis, [(i, i ^ mask) for i in range(lax.axis_size(axis))])


def moved(block, *moves):
    cycle, groups = lax.axis_size("dp"), lax.axis_size("mp")
    route = [
        ((d ^ to ^ source) * groups + (i ^ mask), d * groups + i)
        for to, source, mask in moves
        for d in range(to, cycle, 2)
        for i in range(groups)
    ]
    return lax.ppermute(block, ("dp", "mp"), route)


def after(value, *others):
    return lax.optimization_barrier((value, *others))[0]


def kernel_call(body, out_shape, *args, in_place=(), scratch=(), vmem=SMALL_VMEM):
    return pl.pallas_call(
        body,
        out_shape=out_shape,
        in_specs=[
            pl.BlockSpec(memory_space=pltpu.HBM if i in in_place else pltpu.VMEM) for i in range(len(args))
        ],
        out_specs=jax.tree.map(lambda _: pl.BlockSpec(memory_space=pltpu.VMEM), out_shape),
        scratch_shapes=scratch,
        compiler_params=pltpu.CompilerParams(vmem_limit_bytes=vmem),
    )(*args)


def iota(shape, dimension):
    return lax.broadcasted_iota(jnp.int32, shape, dimension)


def slots_of(owner, groups):
    chains = owner.shape[1]
    marks = (owner == iota((groups, chains), 0)).astype(F32)
    before = (iota((chains, chains), 0) < iota((chains, chains), 1)).astype(BF16)
    counts = jnp.dot(marks.astype(BF16), before, preferred_element_type=F32)
    return marks, jnp.sum(counts * marks, axis=0, keepdims=True)


def request_body(capacity, owner_ref, row_ref, bias_ref, message_ref):
    groups, _, width = message_ref.shape
    bias_count = bias_ref.shape[1]
    marks, rank = slots_of(owner_ref[...], groups)
    ranked = (rank.astype(jnp.int32) == iota((capacity, rank.shape[1]), 0)).astype(F32) * row_ref[...].astype(F32)
    request = lax.dot_general(
        marks.astype(BF16), ranked.astype(BF16), (((1,), (1,)), ((), ())), preferred_element_type=F32
    )
    bias = jnp.broadcast_to(bias_ref[...].astype(F32), (groups, bias_count))
    rest = jnp.zeros((groups, width - bias_count - capacity), F32)
    message_ref[...] = jnp.concatenate([bias, request, rest], axis=1).reshape(message_ref.shape)


def serve_body(capacity, bias_count, message_ref, table_ref, rows_ref):
    groups = message_ref.shape[0]
    slots, held = groups * capacity, table_ref.shape[0]
    message = message_ref[...].reshape(groups, message_ref.shape[2])
    wanted = message[:, bias_count : bias_count + capacity].astype(BF16)
    spread = (iota((slots, groups), 0) // capacity == iota((slots, groups), 1)).astype(BF16)
    by_rank = jnp.dot(spread, wanted, preferred_element_type=F32)
    mine = (iota((slots, capacity), 0) % capacity == iota((slots, capacity), 1)).astype(F32)
    row = jnp.sum(by_rank * mine, axis=1, keepdims=True).astype(jnp.int32)
    pick = (row == iota((slots, held), 1)).astype(BF16)
    rows_ref[...] = jnp.dot(pick, table_ref[...], preferred_element_type=F32).astype(BF16)


def pack_body(capacity, groups, owner_ref, positive_ref, gain_ref, bias_ref, queries_ref, packed_ref):
    chains, features = queries_ref.shape
    owner, positive = owner_ref[...], positive_ref[...]
    _, rank = slots_of(owner, groups)
    slot = owner * capacity + rank.astype(jnp.int32)
    small = jnp.concatenate([slot, positive // DIGIT, positive % DIGIT], axis=0).astype(F32)
    small = jnp.concatenate([small, jnp.zeros((3, features - chains), F32)], axis=1)
    wide = jnp.concatenate([gain_ref[...], bias_ref[...]], axis=0).astype(F32)
    rest = jnp.zeros((TILE_ROWS - 5, features), F32)
    packed_ref[:chains, :] = queries_ref[...]
    packed_ref[chains:, :] = jnp.concatenate([small, wide, rest], axis=0).astype(BF16)


def select_body(packed_ref, fetched_ref, shifted_ref, normed_ref, positive_ref):
    slots = fetched_ref.shape[0]
    chains = shifted_ref.shape[0]
    extra = packed_ref[chains:, :].astype(F32)
    digits = extra[:3, :chains].astype(jnp.int32)
    positive_ref[...] = digits[1:2, :] * DIGIT + digits[2:3, :]
    pick = (digits[0:1, :] == iota((slots, chains), 0)).astype(F32).T.astype(BF16)
    rows = jnp.dot(pick, fetched_ref[...], preferred_element_type=F32)
    combined = packed_ref[:chains, :].astype(F32) + rows
    centred = combined - jnp.mean(combined, axis=1, keepdims=True)
    spread = jnp.mean(centred * centred, axis=1, keepdims=True)
    normed_ref[...] = (centred * lax.rsqrt(spread + 1e-05) * extra[3:4, :]).astype(BF16)
    shifted_ref[...] = combined + extra[4:5, :]


def gelu(u):
    return 0.5 * u * (1.0 + jnp.tanh(0.7978845608028654 * (u + 0.044715 * (u * u * u))))


def hidden_body(plan, normed_ref, normed2_ref, message_ref, *refs):
    shards, (total_ref, total2_ref, held_in, held_out, sems) = refs[:-5], refs[-5:]
    chains, units = total_ref.shape[0], held_in.shape[0] // len(plan)
    me, first_core = lax.axis_index("mp"), lax.axis_index("dp") % 2 == 0
    held = (held_in, held_out)

    def copy(at, p, side):
        return pltpu.make_async_copy(
            shards[at].at[pl.ds(side * units, units)], held[side].at[pl.ds(p * units, units)], sems.at[side, p]
        )

    for side in (0, 1):
        for p, (_, at, _, other_at) in enumerate(plan):
            if at == other_at:
                copy(at, p, side).start()
            else:

                @pl.when(first_core)
                def _():
                    copy(at, p, side).start()

                @pl.when(jnp.logical_not(first_core))
                def _():
                    copy(other_at, p, side).start()

    normed = jnp.concatenate([normed_ref[...], normed2_ref[...]], axis=0)
    places = [me ^ jnp.where(first_core, mask, other_mask) for mask, _, other_mask, _ in plan]
    bias = jnp.concatenate(
        [message_ref[pl.ds(place, 1)].reshape(1, message_ref.shape[2])[:, :units] for place in places], axis=1
    )
    for p, (_, at, _, _) in enumerate(plan):
        copy(at, p, 0).wait()
    preact = lax.dot_general(normed, held_in[...], (((1,), (1,)), ((), ())), preferred_element_type=F32)
    activated = gelu(preact + bias).astype(BF16)
    for p, (_, at, _, _) in enumerate(plan):
        copy(at, p, 1).wait()
    total = jnp.dot(activated, held_out[...], preferred_element_type=F32)
    total_ref[...] = total[:chains, :]
    total2_ref[...] = total[chains:, :].astype(total2_ref.dtype)


def add_body(total_ref, received_ref, sum_ref):
    sum_ref[...] = (total_ref[...] + received_ref[...].astype(F32)).astype(sum_ref.dtype)


def score_body(
    blocks,
    shifted_ref,
    total_ref,
    received_ref,
    other_ref,
    positive_ref,
    *refs,
):
    tools = [ref[...] for ref in refs[:blocks]]
    updated_ref, loss_ref, weights_ref, *grad_refs = refs[blocks:]
    block_rows = tools[0].shape[0]
    branch = total_ref[...] + received_ref[...] + other_ref[...].astype(F32)
    updated = (shifted_ref[...] + branch).astype(BF16)
    updated_ref[...] = updated
    scores = jnp.concatenate(
        [
            lax.dot_general(updated, t, (((1,), (1,)), ((), ())), preferred_element_type=F32)
            for t in tools
        ],
        axis=1,
    )
    tool = iota((scores.shape[1], scores.shape[0]), 0)
    column = ((tool // block_rows) ^ lax.axis_index("dp")) * block_rows + tool % block_rows
    is_positive = (column == positive_ref[...]).astype(F32).T
    row_max = jnp.max(scores, axis=1, keepdims=True)
    log_total = row_max + jnp.log(jnp.sum(jnp.exp(scores - row_max), axis=1, keepdims=True))
    loss_ref[...] = log_total - jnp.sum(scores * is_positive, axis=1, keepdims=True)
    weights = (jnp.exp(scores - log_total) - is_positive).astype(BF16)
    weights_ref[...] = weights
    for block, grad_ref in enumerate(grad_refs):
        grad_ref[...] = lax.dot_general(
            weights[:, block * block_rows : (block + 1) * block_rows],
            updated,
            (((0,), (0,)), ((), ())),
            preferred_element_type=F32,
        ).astype(BF16)


def finish_body(weights_ref, updated_ref, loss_ref, *refs):
    tool_refs, (grad_ref, result_ref, chain_loss_ref) = refs[:-3], refs[-3:]
    result_ref[...] = updated_ref[...]
    chain_loss_ref[...] = loss_ref[...]
    block_rows = tool_refs[0].shape[0]
    grad_ref[...] = sum(
        jnp.dot(
            weights_ref[:, j * block_rows : (j + 1) * block_rows], ref[...], preferred_element_type=F32
        )
        for j, ref in enumerate(tool_refs)
    )


def weight_pieces(own, own_later, groups, hold, asked):
    near = moved(own, (0, 0, 1), (1, 1, 8))
    near_y = moved(own_later, (0, 0, 2))
    first = after(near, asked)
    near, near_y = hold(near, near_y)
    turned = moved(first, (0, 0, 2), (1, 1, 1))
    far_y = moved(first, (1, 1, 2))
    far_both = moved(turned, (1, 1, 2))
    pieces = [(0, own, 8, near), (1, near, 9, turned), (2, near_y, 10, far_y), (3, turned, 11, far_both)]
    for level in range(16, groups, 16):
        base = moved(own, (0, 0, level), (1, 1, level ^ 8))
        by_x, by_y = (moved(base, (0, 0, bit), (1, 1, bit)) for bit in (1, 2))
        both = moved(by_x, (0, 0, 2), (1, 1, 2))
        pieces += [(level ^ m, s, level ^ 8 ^ m, s) for m, s in enumerate((base, by_x, by_y, both))]
    return pieces


def local(
    queries,
    first_owner,
    first_row,
    tool_table,
    norm_gain,
    weight_in,
    bias_in,
    weight_out,
    bias_out,
    tool_embeds,
    positive,
):
    chains, features = queries.shape
    groups, cycle = lax.axis_size("mp"), lax.axis_size("dp")
    capacity = 2 * chains // groups
    slots = groups * capacity
    units = weight_in.shape[0]
    block_rows = tool_embeds.shape[0]
    tool_count = block_rows * cycle

    def whole(shape, dtype):
        return jax.ShapeDtypeStruct(shape, dtype)

    owner_row = first_owner.reshape(1, chains)
    width = -(-(units + capacity) // 128) * 128
    message = kernel_call(
        functools.partial(request_body, capacity),
        whole((groups, 1, width), F32),
        owner_row,
        first_row.reshape(1, chains),
        bias_in.reshape(1, units),
    )
    asked = lax.all_to_all(message, "mp", split_axis=0, concat_axis=0, tiled=True)
    served = kernel_call(
        functools.partial(serve_body, capacity, units),
        whole((slots, features), BF16),
        asked,
        tool_table,
    )
    packed = kernel_call(
        functools.partial(pack_body, capacity, groups),
        whole((chains + TILE_ROWS, features), BF16),
        after(owner_row, served),
        positive.reshape(1, chains),
        norm_gain.reshape(1, features),
        bias_out.reshape(1, features),
        queries,
    )
    own = jnp.concatenate([weight_in, weight_out], axis=0)
    own_later = after(own, message)
    held = []

    def hold(*early):
        early_and_served = lax.optimization_barrier((*early, served))
        held.append(early_and_served[-1])
        return early_and_served[:-1]

    pieces = weight_pieces(own, own_later, groups, hold, asked)
    fetched = lax.all_to_all(held[0], "mp", split_axis=0, concat_axis=0, tiled=True)
    shards = []
    for piece in pieces:
        for shard in (piece[1], piece[3]):
            if all(shard is not s for s in shards):
                shards.append(shard)
    index_of = {id(s): i for i, s in enumerate(shards)}
    plan = tuple((mask, index_of[id(s)], other, index_of[id(t)]) for mask, s, other, t in pieces)

    shifted, normed, positive_row = kernel_call(
        select_body,
        (whole((chains, features), F32), whole((chains, features), BF16), whole((1, chains), jnp.int32)),
        packed,
        fetched,
    )

    def hidden(own_rows, to_share, given):
        return kernel_call(
            functools.partial(hidden_body, plan),
            (whole((chains, features), F32), whole((chains, features), given)),
            own_rows,
            flipped(to_share, "dp", 1),
            asked,
            *shards,
            in_place=range(3, 3 + len(shards)),
            scratch=(
                pltpu.VMEM((len(plan) * units, features), BF16),
                pltpu.VMEM((len(plan) * units, features), BF16),
                pltpu.SemaphoreType.DMA((2, len(plan))),
            ),
            vmem=LARGE_VMEM,
        )

    total, total_for = hidden(normed, after(normed, pieces[2][1]), F32)
    neighbour_normed = after(flipped(normed, "mp", 4), total)
    neighbour, neighbour_for = hidden(neighbour_normed, neighbour_normed, BF16)
    neighbour_sum = kernel_call(
        add_body, whole((chains, features), BF16), neighbour, flipped(neighbour_for, "dp", 1)
    )
    late_tools = after(tool_embeds, total)
    tools = [tool_embeds] + [flipped(late_tools, "dp", j) for j in range(1, cycle)]
    updated, loss, weights, *grads = kernel_call(
        functools.partial(score_body, cycle),
        (
            whole((chains, features), BF16),
            whole((chains, 1), F32),
            whole((chains, tool_count), BF16),
            *(whole((block_rows, features), BF16) for _ in range(cycle)),
        ),
        shifted,
        total,
        flipped(total_for, "dp", 1),
        flipped(neighbour_sum, "mp", 4),
        positive_row,
        *tools,
    )
    query_grad, updated, loss = kernel_call(
        finish_body,
        (whole((chains, features), F32), whole((chains, features), BF16), whole((chains, 1), F32)),
        weights,
        updated,
        loss,
        *tools,
    )

    grad = grads[0].astype(F32)
    for block in range(1, cycle):
        grad = grad + flipped(grads[block], "dp", block).astype(F32)
    bits = [1 << b for b in range((groups - 1).bit_length())]
    turned = bits[len(bits) // 2 :] + bits[: len(bits) // 2]
    for bit, other_bit in zip(bits, turned):
        rounded = grad.astype(BF16)
        grad = rounded.astype(F32) + moved(rounded, (0, 0, bit), (1, 1, other_bit)).astype(F32)
    grad_scale = (tool_count / (chains * groups * cycle)) ** 0.5
    return updated, loss[:, 0], query_grad, grad * grad_scale


def solution(mesh):
    in_specs = (
        P(("dp", "mp"), None),
        P(("dp", "mp"), None),
        P(("dp", "mp")),
        P("mp", None),
        P(),
        P("mp", None),
        P("mp"),
        P("mp", None),
        P(),
        P("dp", None),
        P(("dp", "mp")),
    )
    out_specs = (P(("dp", "mp"), None), P(("dp", "mp")), P(("dp", "mp"), None), P("dp", None))
    return jax.shard_map(local, mesh=mesh, in_specs=in_specs, out_specs=out_specs, check_vma=False)
```

```python
import functools

import jax
import jax.numpy as jnp
from jax import lax
from jax.experimental import pallas as pl
from jax.experimental.pallas import tpu as pltpu
from jax.sharding import PartitionSpec as P

F32 = jnp.float32
BF16 = jnp.bfloat16
DIGIT = 256
TILE_ROWS = 16
SMALL_VMEM = 6 * 1024 * 1024
LARGE_VMEM = 14 * 1024 * 1024


def flipped(block, axis, mask):
    return lax.ppermute(block, axis, [(i, i ^ mask) for i in range(lax.axis_size(axis))])


def moved(block, *moves):
    cycle, groups = lax.axis_size("dp"), lax.axis_size("mp")
    route = [
        ((d ^ to ^ source) * groups + (i ^ mask), d * groups + i)
        for to, source, mask in moves
        for d in range(to, cycle, 2)
        for i in range(groups)
    ]
    return lax.ppermute(block, ("dp", "mp"), route)


def after(value, *others):
    return lax.optimization_barrier((value, *others))[0]


def kernel_call(body, out_shape, *args, in_place=(), scratch=(), vmem=SMALL_VMEM):
    return pl.pallas_call(
        body,
        out_shape=out_shape,
        in_specs=[
            pl.BlockSpec(memory_space=pltpu.HBM if i in in_place else pltpu.VMEM) for i in range(len(args))
        ],
        out_specs=jax.tree.map(lambda _: pl.BlockSpec(memory_space=pltpu.VMEM), out_shape),
        scratch_shapes=scratch,
        compiler_params=pltpu.CompilerParams(vmem_limit_bytes=vmem),
    )(*args)


def iota(shape, dimension):
    return lax.broadcasted_iota(jnp.int32, shape, dimension)


def slots_of(owner, groups):
    chains = owner.shape[1]
    marks = (owner == iota((groups, chains), 0)).astype(F32)
    before = (iota((chains, chains), 0) < iota((chains, chains), 1)).astype(BF16)
    counts = jnp.dot(marks.astype(BF16), before, preferred_element_type=F32)
    return marks, jnp.sum(counts * marks, axis=0, keepdims=True)


def request_body(capacity, owner_ref, row_ref, bias_ref, message_ref):
    groups, _, width = message_ref.shape
    bias_count = bias_ref.shape[1]
    marks, rank = slots_of(owner_ref[...], groups)
    ranked = (rank.astype(jnp.int32) == iota((capacity, rank.shape[1]), 0)).astype(F32) * row_ref[...].astype(F32)
    request = lax.dot_general(
        marks.astype(BF16), ranked.astype(BF16), (((1,), (1,)), ((), ())), preferred_element_type=F32
    )
    bias = jnp.broadcast_to(bias_ref[...].astype(F32), (groups, bias_count))
    rest = jnp.zeros((groups, width - bias_count - capacity), F32)
    message_ref[...] = jnp.concatenate([bias, request, rest], axis=1).reshape(message_ref.shape)


def serve_body(capacity, bias_count, message_ref, table_ref, rows_ref):
    groups = message_ref.shape[0]
    slots, held = groups * capacity, table_ref.shape[0]
    message = message_ref[...].reshape(groups, message_ref.shape[2])
    wanted = message[:, bias_count : bias_count + capacity].astype(BF16)
    spread = (iota((slots, groups), 0) // capacity == iota((slots, groups), 1)).astype(BF16)
    by_rank = jnp.dot(spread, wanted, preferred_element_type=F32)
    mine = (iota((slots, capacity), 0) % capacity == iota((slots, capacity), 1)).astype(F32)
    row = jnp.sum(by_rank * mine, axis=1, keepdims=True).astype(jnp.int32)
    pick = (row == iota((slots, held), 1)).astype(BF16)
    rows_ref[...] = jnp.dot(pick, table_ref[...], preferred_element_type=F32).astype(BF16)


def pack_body(capacity, groups, owner_ref, positive_ref, gain_ref, bias_ref, queries_ref, packed_ref):
    chains, features = queries_ref.shape
    owner, positive = owner_ref[...], positive_ref[...]
    _, rank = slots_of(owner, groups)
    slot = owner * capacity + rank.astype(jnp.int32)
    small = jnp.concatenate([slot, positive // DIGIT, positive % DIGIT], axis=0).astype(F32)
    small = jnp.concatenate([small, jnp.zeros((3, features - chains), F32)], axis=1)
    wide = jnp.concatenate([gain_ref[...], bias_ref[...]], axis=0).astype(F32)
    rest = jnp.zeros((TILE_ROWS - 5, features), F32)
    packed_ref[:chains, :] = queries_ref[...]
    packed_ref[chains:, :] = jnp.concatenate([small, wide, rest], axis=0).astype(BF16)


def select_body(packed_ref, fetched_ref, shifted_ref, normed_ref, positive_ref):
    slots = fetched_ref.shape[0]
    chains = shifted_ref.shape[0]
    extra = packed_ref[chains:, :].astype(F32)
    digits = extra[:3, :chains].astype(jnp.int32)
    positive_ref[...] = digits[1:2, :] * DIGIT + digits[2:3, :]
    pick = (digits[0:1, :] == iota((slots, chains), 0)).astype(F32).T.astype(BF16)
    rows = jnp.dot(pick, fetched_ref[...], preferred_element_type=F32)
    combined = packed_ref[:chains, :].astype(F32) + rows
    centred = combined - jnp.mean(combined, axis=1, keepdims=True)
    spread = jnp.mean(centred * centred, axis=1, keepdims=True)
    normed_ref[...] = (centred * lax.rsqrt(spread + 1e-05) * extra[3:4, :]).astype(BF16)
    shifted_ref[...] = combined + extra[4:5, :]


def gelu(u):
    return 0.5 * u * (1.0 + jnp.tanh(0.7978845608028654 * (u + 0.044715 * (u * u * u))))


def hidden_body(plan, normed_ref, message_ref, *refs):
    shards, (total_ref, held_in, held_out, sems) = refs[:-4], refs[-4:]
    units = held_in.shape[0] // len(plan)
    me, first_core = lax.axis_index("mp"), lax.axis_index("dp") % 2 == 0
    held = (held_in, held_out)

    def copy(at, p, side):
        return pltpu.make_async_copy(
            shards[at].at[pl.ds(side * units, units)], held[side].at[pl.ds(p * units, units)], sems.at[side, p]
        )

    for side in (0, 1):
        for p, (_, at, _, other_at) in enumerate(plan):
            if at == other_at:
                copy(at, p, side).start()
            else:

                @pl.when(first_core)
                def _():
                    copy(at, p, side).start()

                @pl.when(jnp.logical_not(first_core))
                def _():
                    copy(other_at, p, side).start()

    normed = normed_ref[...]
    places = [me ^ jnp.where(first_core, mask, other_mask) for mask, _, other_mask, _ in plan]
    bias = jnp.concatenate(
        [message_ref[pl.ds(place, 1)].reshape(1, message_ref.shape[2])[:, :units] for place in places], axis=1
    )
    for p, (_, at, _, _) in enumerate(plan):
        copy(at, p, 0).wait()
    preact = lax.dot_general(normed, held_in[...], (((1,), (1,)), ((), ())), preferred_element_type=F32)
    activated = gelu(preact + bias).astype(BF16)
    for p, (_, at, _, _) in enumerate(plan):
        copy(at, p, 1).wait()
    total_ref[...] = jnp.dot(activated, held_out[...], preferred_element_type=F32).astype(total_ref.dtype)


def score_body(
    blocks,
    shifted_ref,
    total_ref,
    other_ref,
    positive_ref,
    *refs,
):
    tools = [ref[...] for ref in refs[:blocks]]
    updated_ref, loss_ref, weights_ref, *grad_refs = refs[blocks:]
    block_rows = tools[0].shape[0]
    branch = total_ref[...] + other_ref[...].astype(F32)
    updated = (shifted_ref[...] + branch).astype(BF16)
    updated_ref[...] = updated
    scores = jnp.concatenate(
        [
            lax.dot_general(updated, t, (((1,), (1,)), ((), ())), preferred_element_type=F32)
            for t in tools
        ],
        axis=1,
    )
    tool = iota((scores.shape[1], scores.shape[0]), 0)
    column = ((tool // block_rows) ^ lax.axis_index("dp")) * block_rows + tool % block_rows
    is_positive = (column == positive_ref[...]).astype(F32).T
    row_max = jnp.max(scores, axis=1, keepdims=True)
    log_total = row_max + jnp.log(jnp.sum(jnp.exp(scores - row_max), axis=1, keepdims=True))
    loss_ref[...] = log_total - jnp.sum(scores * is_positive, axis=1, keepdims=True)
    weights = (jnp.exp(scores - log_total) - is_positive).astype(BF16)
    weights_ref[...] = weights
    for block, grad_ref in enumerate(grad_refs):
        grad_ref[...] = lax.dot_general(
            weights[:, block * block_rows : (block + 1) * block_rows],
            updated,
            (((0,), (0,)), ((), ())),
            preferred_element_type=F32,
        ).astype(BF16)


def finish_body(weights_ref, updated_ref, loss_ref, *refs):
    tool_refs, (grad_ref, result_ref, chain_loss_ref) = refs[:-3], refs[-3:]
    result_ref[...] = updated_ref[...]
    chain_loss_ref[...] = loss_ref[...]
    block_rows = tool_refs[0].shape[0]
    grad_ref[...] = sum(
        jnp.dot(
            weights_ref[:, j * block_rows : (j + 1) * block_rows], ref[...], preferred_element_type=F32
        )
        for j, ref in enumerate(tool_refs)
    )


def weight_pieces(own, own_later, groups, hold, asked):
    near = moved(own, (0, 0, 1), (1, 1, 8))
    near_y = moved(own_later, (0, 0, 2))
    first = after(near, asked)
    near, near_y = hold(near, near_y)
    turned = moved(first, (0, 0, 2), (1, 1, 1))
    far_y = moved(first, (1, 1, 2))
    far_both = moved(turned, (1, 1, 2))
    levels = []
    for level in range(16, groups, 16):
        base = moved(own, (0, 0, level), (1, 1, level ^ 8))
        by_x, by_y = (moved(base, (0, 0, bit), (1, 1, bit)) for bit in (1, 2))
        both = moved(by_x, (0, 0, 2), (1, 1, 2))
        levels += [(level ^ m, shard, level ^ 8 ^ m) for m, shard in enumerate((base, by_x, by_y, both))]
    return [(1, near, 8), (3, turned, 9), *levels], (near_y, far_y, far_both)


def shared_pieces(own, symmetric, near_y, far_y, far_both, ready):
    pieces = [(0, own, 0, own)]
    for mask, shard, other_mask in symmetric:
        given = flipped(after(shard, ready), "dp", 1)
        pieces += [(mask, shard, other_mask, shard), (other_mask, given, mask, given)]
    pieces.append((2, near_y, 2, flipped(after(near_y, ready), "dp", 1)))
    pieces.append((10, flipped(after(far_y, ready), "dp", 1), 10, far_y))
    pieces.append((11, flipped(after(far_both, ready), "dp", 1), 11, far_both))
    return pieces


def local(
    queries,
    first_owner,
    first_row,
    tool_table,
    norm_gain,
    weight_in,
    bias_in,
    weight_out,
    bias_out,
    tool_embeds,
    positive,
):
    chains, features = queries.shape
    groups, cycle = lax.axis_size("mp"), lax.axis_size("dp")
    capacity = 2 * chains // groups
    slots = groups * capacity
    units = weight_in.shape[0]
    block_rows = tool_embeds.shape[0]
    tool_count = block_rows * cycle

    def whole(shape, dtype):
        return jax.ShapeDtypeStruct(shape, dtype)

    owner_row = first_owner.reshape(1, chains)
    width = -(-(units + capacity) // 128) * 128
    message = kernel_call(
        functools.partial(request_body, capacity),
        whole((groups, 1, width), F32),
        owner_row,
        first_row.reshape(1, chains),
        bias_in.reshape(1, units),
    )
    asked = lax.all_to_all(message, "mp", split_axis=0, concat_axis=0, tiled=True)
    served = kernel_call(
        functools.partial(serve_body, capacity, units),
        whole((slots, features), BF16),
        asked,
        tool_table,
    )
    packed = kernel_call(
        functools.partial(pack_body, capacity, groups),
        whole((chains + TILE_ROWS, features), BF16),
        after(owner_row, served),
        positive.reshape(1, chains),
        norm_gain.reshape(1, features),
        bias_out.reshape(1, features),
        queries,
    )
    own = jnp.concatenate([weight_in, weight_out], axis=0)
    own_later = after(own, message)
    held = []

    def hold(*early):
        early_and_served = lax.optimization_barrier((*early, served))
        held.append(early_and_served[-1])
        return early_and_served[:-1]

    symmetric, single = weight_pieces(own, own_later, groups, hold, asked)
    fetched = lax.all_to_all(held[0], "mp", split_axis=0, concat_axis=0, tiled=True)
    shifted, normed, positive_row = kernel_call(
        select_body,
        (whole((chains, features), F32), whole((chains, features), BF16), whole((1, chains), jnp.int32)),
        packed,
        fetched,
    )

    pieces = shared_pieces(own, symmetric, *single, normed)
    shards = []
    for piece in pieces:
        for shard in (piece[1], piece[3]):
            if all(shard is not s for s in shards):
                shards.append(shard)
    index_of = {id(s): i for i, s in enumerate(shards)}
    plan = tuple((mask, index_of[id(s)], other, index_of[id(t)]) for mask, s, other, t in pieces)

    def hidden(rows, held_as):
        return kernel_call(
            functools.partial(hidden_body, plan),
            whole((chains, features), held_as),
            rows,
            asked,
            *shards,
            in_place=range(2, 2 + len(shards)),
            scratch=(
                pltpu.VMEM((len(plan) * units, features), BF16),
                pltpu.VMEM((len(plan) * units, features), BF16),
                pltpu.SemaphoreType.DMA((2, len(plan))),
            ),
            vmem=LARGE_VMEM,
        )

    neighbour = hidden(flipped(normed, "mp", 4), BF16)
    total = hidden(after(normed, neighbour), F32)
    late_tools = after(tool_embeds, neighbour)
    tools = [tool_embeds] + [flipped(late_tools, "dp", j) for j in range(1, cycle)]
    updated, loss, weights, *grads = kernel_call(
        functools.partial(score_body, cycle),
        (
            whole((chains, features), BF16),
            whole((chains, 1), F32),
            whole((chains, tool_count), BF16),
            *(whole((block_rows, features), BF16) for _ in range(cycle)),
        ),
        shifted,
        total,
        flipped(neighbour, "mp", 4),
        positive_row,
        *tools,
    )
    query_grad, updated, loss = kernel_call(
        finish_body,
        (whole((chains, features), F32), whole((chains, features), BF16), whole((chains, 1), F32)),
        weights,
        updated,
        loss,
        *tools,
    )

    grad = grads[0].astype(F32)
    for block in range(1, cycle):
        grad = grad + flipped(grads[block], "dp", block).astype(F32)
    bits = [1 << b for b in range((groups - 1).bit_length())]
    turned = bits[len(bits) // 2 :] + bits[: len(bits) // 2]
    for bit, other_bit in zip(bits, turned):
        rounded = grad.astype(BF16)
        grad = rounded.astype(F32) + moved(rounded, (0, 0, bit), (1, 1, other_bit)).astype(F32)
    grad_scale = (tool_count / (chains * groups * cycle)) ** 0.5
    return updated, loss[:, 0], query_grad, grad * grad_scale


def solution(mesh):
    in_specs = (
        P(("dp", "mp"), None),
        P(("dp", "mp"), None),
        P(("dp", "mp")),
        P("mp", None),
        P(),
        P("mp", None),
        P("mp"),
        P("mp", None),
        P(),
        P("dp", None),
        P(("dp", "mp")),
    )
    out_specs = (P(("dp", "mp"), None), P(("dp", "mp")), P(("dp", "mp"), None), P("dp", None))
    return jax.shard_map(local, mesh=mesh, in_specs=in_specs, out_specs=out_specs, check_vma=False)
```

```python
import functools

import jax
import jax.numpy as jnp
from jax import lax
from jax.experimental import pallas as pl
from jax.experimental.pallas import tpu as pltpu
from jax.sharding import PartitionSpec as P

F32 = jnp.float32
BF16 = jnp.bfloat16
DIGIT = 256
TILE_ROWS = 16
SMALL_VMEM = 6 * 1024 * 1024
LARGE_VMEM = 14 * 1024 * 1024


def flipped(block, axis, mask):
    return lax.ppermute(block, axis, [(i, i ^ mask) for i in range(lax.axis_size(axis))])


def moved(block, *moves):
    cycle, groups = lax.axis_size("dp"), lax.axis_size("mp")
    route = [
        ((d ^ to ^ source) * groups + (i ^ mask), d * groups + i)
        for to, source, mask in moves
        for d in range(to, cycle, 2)
        for i in range(groups)
    ]
    return lax.ppermute(block, ("dp", "mp"), route)


def after(value, *others):
    return lax.optimization_barrier((value, *others))[0]


def kernel_call(body, out_shape, *args, in_place=(), scratch=(), vmem=SMALL_VMEM):
    return pl.pallas_call(
        body,
        out_shape=out_shape,
        in_specs=[
            pl.BlockSpec(memory_space=pltpu.HBM if i in in_place else pltpu.VMEM) for i in range(len(args))
        ],
        out_specs=jax.tree.map(lambda _: pl.BlockSpec(memory_space=pltpu.VMEM), out_shape),
        scratch_shapes=scratch,
        compiler_params=pltpu.CompilerParams(vmem_limit_bytes=vmem),
    )(*args)


def iota(shape, dimension):
    return lax.broadcasted_iota(jnp.int32, shape, dimension)


def slots_of(owner, groups):
    chains = owner.shape[1]
    marks = (owner == iota((groups, chains), 0)).astype(F32)
    before = (iota((chains, chains), 0) < iota((chains, chains), 1)).astype(BF16)
    counts = jnp.dot(marks.astype(BF16), before, preferred_element_type=F32)
    return marks, jnp.sum(counts * marks, axis=0, keepdims=True)


def request_body(capacity, owner_ref, row_ref, bias_ref, message_ref):
    groups, _, width = message_ref.shape
    bias_count = bias_ref.shape[0]
    marks, rank = slots_of(owner_ref[...], groups)
    ranked = (rank.astype(jnp.int32) == iota((capacity, rank.shape[1]), 0)).astype(F32) * row_ref[...].astype(F32)
    request = lax.dot_general(
        marks.astype(BF16), ranked.astype(BF16), (((1,), (1,)), ((), ())), preferred_element_type=F32
    )
    bias = jnp.broadcast_to(bias_ref[...].astype(F32)[None, :], (groups, bias_count))
    rest = jnp.zeros((groups, width - bias_count - capacity), F32)
    message_ref[...] = jnp.concatenate([bias, request, rest], axis=1).reshape(message_ref.shape)


def serve_body(capacity, bias_count, message_ref, table_ref, rows_ref):
    groups = message_ref.shape[0]
    slots, held = groups * capacity, table_ref.shape[0]
    message = message_ref[...].reshape(groups, message_ref.shape[2])
    wanted = message[:, bias_count : bias_count + capacity].astype(BF16)
    spread = (iota((slots, groups), 0) // capacity == iota((slots, groups), 1)).astype(BF16)
    by_rank = jnp.dot(spread, wanted, preferred_element_type=F32)
    mine = (iota((slots, capacity), 0) % capacity == iota((slots, capacity), 1)).astype(F32)
    row = jnp.sum(by_rank * mine, axis=1, keepdims=True).astype(jnp.int32)
    pick = (row == iota((slots, held), 1)).astype(BF16)
    rows_ref[...] = jnp.dot(pick, table_ref[...], preferred_element_type=F32).astype(BF16)


def pack_body(capacity, groups, owner_ref, positive_ref, gain_ref, bias_ref, queries_ref, packed_ref):
    chains, features = queries_ref.shape
    owner, positive = owner_ref[...], positive_ref[...]
    _, rank = slots_of(owner, groups)
    slot = owner * capacity + rank.astype(jnp.int32)
    small = jnp.concatenate([slot, positive // DIGIT, positive % DIGIT], axis=0).astype(F32)
    small = jnp.concatenate([small, jnp.zeros((3, features - chains), F32)], axis=1)
    wide = jnp.concatenate([ref[...].astype(F32)[None, :] for ref in (gain_ref, bias_ref)], axis=0)
    rest = jnp.zeros((TILE_ROWS - 5, features), F32)
    packed_ref[:chains, :] = queries_ref[...]
    packed_ref[chains:, :] = jnp.concatenate([small, wide, rest], axis=0).astype(BF16)


def select_body(packed_ref, fetched_ref, shifted_ref, normed_ref, positive_ref):
    slots = fetched_ref.shape[0]
    chains = shifted_ref.shape[0]
    extra = packed_ref[chains:, :].astype(F32)
    digits = extra[:3, :chains].astype(jnp.int32)
    positive_ref[...] = digits[1:2, :] * DIGIT + digits[2:3, :]
    pick = (digits[0:1, :] == iota((slots, chains), 0)).astype(F32).T.astype(BF16)
    rows = jnp.dot(pick, fetched_ref[...], preferred_element_type=F32)
    combined = packed_ref[:chains, :].astype(F32) + rows
    centred = combined - jnp.mean(combined, axis=1, keepdims=True)
    spread = jnp.mean(centred * centred, axis=1, keepdims=True)
    normed_ref[...] = (centred * lax.rsqrt(spread + 1e-05) * extra[3:4, :]).astype(BF16)
    shifted_ref[...] = combined + extra[4:5, :]


def gelu(u):
    return 0.5 * u * (1.0 + jnp.tanh(0.7978845608028654 * (u + 0.044715 * (u * u * u))))


def hidden_body(plan, continued, normed_ref, message_ref, *refs):
    sums, shards, (total_ref, held_in, held_out, sems) = refs[:continued], refs[continued:-4], refs[-4:]
    units = held_in.shape[0] // len(plan)
    me, first_core = lax.axis_index("mp"), lax.axis_index("dp") % 2 == 0
    held = (held_in, held_out)

    def copy(at, p, side):
        return pltpu.make_async_copy(
            shards[at].at[pl.ds(side * units, units)], held[side].at[pl.ds(p * units, units)], sems.at[side, p]
        )

    for side in (0, 1):
        for p, (_, at, _, other_at) in enumerate(plan):
            if at == other_at:
                copy(at, p, side).start()
            else:

                @pl.when(first_core)
                def _():
                    copy(at, p, side).start()

                @pl.when(jnp.logical_not(first_core))
                def _():
                    copy(other_at, p, side).start()

    normed = normed_ref[...]
    places = [me ^ jnp.where(first_core, mask, other_mask) for mask, _, other_mask, _ in plan]
    bias = jnp.concatenate(
        [message_ref[pl.ds(place, 1)].reshape(1, message_ref.shape[2])[:, :units] for place in places], axis=1
    )
    for p, (_, at, _, _) in enumerate(plan):
        copy(at, p, 0).wait()
    preact = lax.dot_general(normed, held_in[...], (((1,), (1,)), ((), ())), preferred_element_type=F32)
    activated = gelu(preact + bias).astype(BF16)
    for p, (_, at, _, _) in enumerate(plan):
        copy(at, p, 1).wait()
    total = jnp.dot(activated, held_out[...], preferred_element_type=F32)
    for sum_ref in sums:
        total = total + sum_ref[...]
    total_ref[...] = total.astype(total_ref.dtype)


def score_body(
    blocks,
    shifted_ref,
    total_ref,
    other_ref,
    positive_ref,
    *refs,
):
    tools = [ref[...] for ref in refs[:blocks]]
    updated_ref, loss_ref, weights_ref, *grad_refs = refs[blocks:]
    block_rows = tools[0].shape[0]
    branch = total_ref[...] + other_ref[...].astype(F32)
    updated = (shifted_ref[...] + branch).astype(BF16)
    updated_ref[...] = updated
    scores = jnp.concatenate(
        [
            lax.dot_general(updated, t, (((1,), (1,)), ((), ())), preferred_element_type=F32)
            for t in tools
        ],
        axis=1,
    )
    tool = iota((scores.shape[1], scores.shape[0]), 0)
    column = ((tool // block_rows) ^ lax.axis_index("dp")) * block_rows + tool % block_rows
    is_positive = (column == positive_ref[...]).astype(F32).T
    row_max = jnp.max(scores, axis=1, keepdims=True)
    log_total = row_max + jnp.log(jnp.sum(jnp.exp(scores - row_max), axis=1, keepdims=True))
    loss_ref[...] = log_total - jnp.sum(scores * is_positive, axis=1, keepdims=True)
    weights = (jnp.exp(scores - log_total) - is_positive).astype(BF16)
    weights_ref[...] = weights
    for block, grad_ref in enumerate(grad_refs):
        grad_ref[...] = lax.dot_general(
            weights[:, block * block_rows : (block + 1) * block_rows],
            updated,
            (((0,), (0,)), ((), ())),
            preferred_element_type=F32,
        ).astype(BF16)


def finish_body(weights_ref, updated_ref, loss_ref, *refs):
    tool_refs, (grad_ref, result_ref, chain_loss_ref) = refs[:-3], refs[-3:]
    result_ref[...] = updated_ref[...]
    chain_loss_ref[...] = loss_ref[...]
    block_rows = tool_refs[0].shape[0]
    grad_ref[...] = sum(
        jnp.dot(
            weights_ref[:, j * block_rows : (j + 1) * block_rows], ref[...], preferred_element_type=F32
        )
        for j, ref in enumerate(tool_refs)
    )


def weight_pieces(own, own_later, groups, hold, asked):
    near = moved(own, (0, 0, 1), (1, 1, 8))
    near_y = moved(own_later, (0, 0, 2))
    first = after(near, asked)
    near, near_y = hold(near, near_y)
    turned = moved(first, (0, 0, 2), (1, 1, 1))
    far_y = moved(first, (1, 1, 2))
    far_both = moved(turned, (1, 1, 2))
    levels = []
    for level in range(16, groups, 16):
        base = moved(own, (0, 0, level), (1, 1, level ^ 8))
        by_x, by_y = (moved(base, (0, 0, bit), (1, 1, bit)) for bit in (1, 2))
        both = moved(by_x, (0, 0, 2), (1, 1, 2))
        levels += [(level ^ m, shard, level ^ 8 ^ m) for m, shard in enumerate((base, by_x, by_y, both))]
    return [(1, near, 8), (3, turned, 9), *levels], (near_y, far_y, far_both)


def shared_pieces(own, symmetric, near_y, far_y, far_both, ready):
    pieces = [(0, own, 0, own)]
    for mask, shard, other_mask in symmetric:
        given = flipped(after(shard, ready), "dp", 1)
        pieces += [(mask, shard, other_mask, shard), (other_mask, given, mask, given)]
    pieces.append((2, near_y, 2, flipped(after(near_y, ready), "dp", 1)))
    pieces.append((10, flipped(after(far_y, ready), "dp", 1), 10, far_y))
    pieces.append((11, flipped(after(far_both, ready), "dp", 1), 11, far_both))
    return pieces


def local(
    queries,
    first_owner,
    first_row,
    tool_table,
    norm_gain,
    weight_in,
    bias_in,
    weight_out,
    bias_out,
    tool_embeds,
    positive,
):
    chains, features = queries.shape
    groups, cycle = lax.axis_size("mp"), lax.axis_size("dp")
    capacity = 2 * chains // groups
    slots = groups * capacity
    units = weight_in.shape[0]
    block_rows = tool_embeds.shape[0]
    tool_count = block_rows * cycle

    def whole(shape, dtype):
        return jax.ShapeDtypeStruct(shape, dtype)

    owner_row = first_owner.reshape(1, chains)
    width = -(-(units + capacity) // 128) * 128
    message = kernel_call(
        functools.partial(request_body, capacity),
        whole((groups, 1, width), F32),
        owner_row,
        first_row.reshape(1, chains),
        bias_in,
    )
    asked = lax.all_to_all(message, "mp", split_axis=0, concat_axis=0, tiled=True)
    served = kernel_call(
        functools.partial(serve_body, capacity, units),
        whole((slots, features), BF16),
        asked,
        tool_table,
    )
    packed = kernel_call(
        functools.partial(pack_body, capacity, groups),
        whole((chains + TILE_ROWS, features), BF16),
        after(owner_row, served),
        positive.reshape(1, chains),
        norm_gain,
        bias_out,
        queries,
    )
    own = jnp.concatenate([weight_in, weight_out], axis=0)
    own_later = after(own, message)
    held = []

    def hold(*early):
        early_and_served = lax.optimization_barrier((*early, served))
        held.append(early_and_served[-1])
        return early_and_served[:-1]

    symmetric, single = weight_pieces(own, own_later, groups, hold, asked)
    fetched = lax.all_to_all(held[0], "mp", split_axis=0, concat_axis=0, tiled=True)
    shifted, normed, positive_row = kernel_call(
        select_body,
        (whole((chains, features), F32), whole((chains, features), BF16), whole((1, chains), jnp.int32)),
        packed,
        fetched,
    )

    pieces = shared_pieces(own, symmetric, *single, normed)
    def hidden(rows, some, held_as, *so_far):
        shards = []
        for piece in some:
            for shard in (piece[1], piece[3]):
                if all(shard is not s for s in shards):
                    shards.append(shard)
        index_of = {id(s): i for i, s in enumerate(shards)}
        plan = tuple((mask, index_of[id(s)], other, index_of[id(t)]) for mask, s, other, t in some)
        first = 2 + len(so_far)
        return kernel_call(
            functools.partial(hidden_body, plan, len(so_far)),
            whole((chains, features), held_as),
            rows,
            asked,
            *so_far,
            *shards,
            in_place=range(first, first + len(shards)),
            scratch=(
                pltpu.VMEM((len(plan) * units, features), BF16),
                pltpu.VMEM((len(plan) * units, features), BF16),
                pltpu.SemaphoreType.DMA((2, len(plan))),
            ),
            vmem=LARGE_VMEM,
        )

    neighbour_normed = flipped(normed, "mp", 4)
    neighbour = hidden(
        neighbour_normed, pieces[-1:], BF16, hidden(neighbour_normed, pieces[:-1], F32)
    )
    total = hidden(after(normed, neighbour), pieces, F32)
    late_tools = after(tool_embeds, neighbour)
    tools = [tool_embeds] + [flipped(late_tools, "dp", j) for j in range(1, cycle)]
    updated, loss, weights, *grads = kernel_call(
        functools.partial(score_body, cycle),
        (
            whole((chains, features), BF16),
            whole((chains, 1), F32),
            whole((chains, tool_count), BF16),
            *(whole((block_rows, features), BF16) for _ in range(cycle)),
        ),
        shifted,
        total,
        flipped(neighbour, "mp", 4),
        positive_row,
        *tools,
    )
    query_grad, updated, loss = kernel_call(
        finish_body,
        (whole((chains, features), F32), whole((chains, features), BF16), whole((chains, 1), F32)),
        weights,
        updated,
        loss,
        *tools,
    )

    grad = grads[0].astype(F32)
    for block in range(1, cycle):
        grad = grad + flipped(grads[block], "dp", block).astype(F32)
    bits = [1 << b for b in range((groups - 1).bit_length())]
    turned = bits[len(bits) // 2 :] + bits[: len(bits) // 2]
    for bit, other_bit in zip(bits, turned):
        rounded = grad.astype(BF16)
        grad = rounded.astype(F32) + moved(rounded, (0, 0, bit), (1, 1, other_bit)).astype(F32)
    grad_scale = (tool_count / (chains * groups * cycle)) ** 0.5
    return updated, loss[:, 0], query_grad, grad * grad_scale


def solution(mesh):
    in_specs = (
        P(("dp", "mp"), None),
        P(("dp", "mp"), None),
        P(("dp", "mp")),
        P("mp", None),
        P(),
        P("mp", None),
        P("mp"),
        P("mp", None),
        P(),
        P("dp", None),
        P(("dp", "mp")),
    )
    out_specs = (P(("dp", "mp"), None), P(("dp", "mp")), P(("dp", "mp"), None), P("dp", None))
    return jax.shard_map(local, mesh=mesh, in_specs=in_specs, out_specs=out_specs, check_vma=False)
```

```python
import functools

import jax
import jax.numpy as jnp
from jax import lax
from jax.experimental import pallas as pl
from jax.experimental.pallas import tpu as pltpu
from jax.sharding import PartitionSpec as P

F32 = jnp.float32
BF16 = jnp.bfloat16
DIGIT = 256
TILE_ROWS = 16
SMALL_VMEM = 6 * 1024 * 1024
LARGE_VMEM = 14 * 1024 * 1024


def flipped(block, axis, mask):
    return lax.ppermute(block, axis, [(i, i ^ mask) for i in range(lax.axis_size(axis))])


def moved(block, *moves):
    cycle, groups = lax.axis_size("dp"), lax.axis_size("mp")
    route = [
        ((d ^ to ^ source) * groups + (i ^ mask), d * groups + i)
        for to, source, mask in moves
        for d in range(to, cycle, 2)
        for i in range(groups)
    ]
    return lax.ppermute(block, ("dp", "mp"), route)


def after(value, *others):
    return lax.optimization_barrier((value, *others))[0]


def kernel_call(body, out_shape, *args, in_place=(), scratch=(), vmem=SMALL_VMEM):
    return pl.pallas_call(
        body,
        out_shape=out_shape,
        in_specs=[
            pl.BlockSpec(memory_space=pltpu.HBM if i in in_place else pltpu.VMEM) for i in range(len(args))
        ],
        out_specs=jax.tree.map(lambda _: pl.BlockSpec(memory_space=pltpu.VMEM), out_shape),
        scratch_shapes=scratch,
        compiler_params=pltpu.CompilerParams(vmem_limit_bytes=vmem),
    )(*args)


def iota(shape, dimension):
    return lax.broadcasted_iota(jnp.int32, shape, dimension)


def slots_of(owner, groups):
    chains = owner.shape[1]
    marks = (owner == iota((groups, chains), 0)).astype(F32)
    before = (iota((chains, chains), 0) < iota((chains, chains), 1)).astype(BF16)
    counts = jnp.dot(marks.astype(BF16), before, preferred_element_type=F32)
    return marks, jnp.sum(counts * marks, axis=0, keepdims=True)


def request_body(capacity, owner_ref, row_ref, bias_ref, message_ref):
    groups, _, width = message_ref.shape
    bias_count = bias_ref.shape[0]
    marks, rank = slots_of(owner_ref[...], groups)
    ranked = (rank.astype(jnp.int32) == iota((capacity, rank.shape[1]), 0)).astype(F32) * row_ref[...].astype(F32)
    request = lax.dot_general(
        marks.astype(BF16), ranked.astype(BF16), (((1,), (1,)), ((), ())), preferred_element_type=F32
    )
    bias = jnp.broadcast_to(bias_ref[...].astype(F32)[None, :], (groups, bias_count))
    rest = jnp.zeros((groups, width - bias_count - capacity), F32)
    message_ref[...] = jnp.concatenate([bias, request, rest], axis=1).reshape(message_ref.shape)


def serve_body(capacity, bias_count, message_ref, table_ref, rows_ref):
    groups = message_ref.shape[0]
    slots, held = groups * capacity, table_ref.shape[0]
    message = message_ref[...].reshape(groups, message_ref.shape[2])
    wanted = message[:, bias_count : bias_count + capacity].astype(BF16)
    spread = (iota((slots, groups), 0) // capacity == iota((slots, groups), 1)).astype(BF16)
    by_rank = jnp.dot(spread, wanted, preferred_element_type=F32)
    mine = (iota((slots, capacity), 0) % capacity == iota((slots, capacity), 1)).astype(F32)
    row = jnp.sum(by_rank * mine, axis=1, keepdims=True).astype(jnp.int32)
    pick = (row == iota((slots, held), 1)).astype(BF16)
    rows_ref[...] = jnp.dot(pick, table_ref[...], preferred_element_type=F32).astype(BF16)


def pack_body(capacity, groups, owner_ref, positive_ref, gain_ref, bias_ref, queries_ref, packed_ref):
    chains, features = queries_ref.shape
    owner, positive = owner_ref[...], positive_ref[...]
    _, rank = slots_of(owner, groups)
    slot = owner * capacity + rank.astype(jnp.int32)
    small = jnp.concatenate([slot, positive // DIGIT, positive % DIGIT], axis=0).astype(F32)
    small = jnp.concatenate([small, jnp.zeros((3, features - chains), F32)], axis=1)
    wide = jnp.concatenate([ref[...].astype(F32)[None, :] for ref in (gain_ref, bias_ref)], axis=0)
    rest = jnp.zeros((TILE_ROWS - 5, features), F32)
    packed_ref[:chains, :] = queries_ref[...]
    packed_ref[chains:, :] = jnp.concatenate([small, wide, rest], axis=0).astype(BF16)


def select_body(packed_ref, fetched_ref, shifted_ref, normed_ref, positive_ref):
    slots = fetched_ref.shape[0]
    chains = shifted_ref.shape[0]
    extra = packed_ref[chains:, :].astype(F32)
    digits = extra[:3, :chains].astype(jnp.int32)
    positive_ref[...] = digits[1:2, :] * DIGIT + digits[2:3, :]
    pick = (digits[0:1, :] == iota((slots, chains), 0)).astype(F32).T.astype(BF16)
    rows = jnp.dot(pick, fetched_ref[...], preferred_element_type=F32)
    combined = packed_ref[:chains, :].astype(F32) + rows
    centred = combined - jnp.mean(combined, axis=1, keepdims=True)
    spread = jnp.mean(centred * centred, axis=1, keepdims=True)
    normed_ref[...] = (centred * lax.rsqrt(spread + 1e-05) * extra[3:4, :]).astype(BF16)
    shifted_ref[...] = combined + extra[4:5, :]


def gelu(u):
    return 0.5 * u * (1.0 + jnp.tanh(0.7978845608028654 * (u + 0.044715 * (u * u * u))))


def hidden_body(plan, continued, normed_ref, message_ref, *refs):
    sums, shards, (total_ref, held_in, held_out, sems) = refs[:continued], refs[continued:-4], refs[-4:]
    units = held_in.shape[0] // len(plan)
    me, first_core = lax.axis_index("mp"), lax.axis_index("dp") % 2 == 0
    held = (held_in, held_out)

    def copy(at, p, side):
        return pltpu.make_async_copy(
            shards[at].at[pl.ds(side * units, units)], held[side].at[pl.ds(p * units, units)], sems.at[side, p]
        )

    for side in (0, 1):
        for p, (_, at, _, other_at) in enumerate(plan):
            if at == other_at:
                copy(at, p, side).start()
            else:

                @pl.when(first_core)
                def _():
                    copy(at, p, side).start()

                @pl.when(jnp.logical_not(first_core))
                def _():
                    copy(other_at, p, side).start()

    normed = normed_ref[...]
    places = [me ^ jnp.where(first_core, mask, other_mask) for mask, _, other_mask, _ in plan]
    bias = jnp.concatenate(
        [message_ref[pl.ds(place, 1)].reshape(1, message_ref.shape[2])[:, :units] for place in places], axis=1
    )
    for p, (_, at, _, _) in enumerate(plan):
        copy(at, p, 0).wait()
    preact = lax.dot_general(normed, held_in[...], (((1,), (1,)), ((), ())), preferred_element_type=F32)
    activated = gelu(preact + bias).astype(BF16)
    for p, (_, at, _, _) in enumerate(plan):
        copy(at, p, 1).wait()
    total = jnp.dot(activated, held_out[...], preferred_element_type=F32)
    for sum_ref in sums:
        total = total + sum_ref[...]
    total_ref[...] = total.astype(total_ref.dtype)


def score_body(
    blocks,
    shifted_ref,
    total_ref,
    other_ref,
    positive_ref,
    *refs,
):
    tools = [ref[...] for ref in refs[:blocks]]
    updated_ref, loss_ref, weights_ref, *grad_refs = refs[blocks:]
    block_rows = tools[0].shape[0]
    branch = total_ref[...] + other_ref[...].astype(F32)
    updated = (shifted_ref[...] + branch).astype(BF16)
    updated_ref[...] = updated
    scores = jnp.concatenate(
        [
            lax.dot_general(updated, t, (((1,), (1,)), ((), ())), preferred_element_type=F32)
            for t in tools
        ],
        axis=1,
    )
    tool = iota((scores.shape[1], scores.shape[0]), 0)
    column = ((tool // block_rows) ^ lax.axis_index("dp")) * block_rows + tool % block_rows
    is_positive = (column == positive_ref[...]).astype(F32).T
    row_max = jnp.max(scores, axis=1, keepdims=True)
    log_total = row_max + jnp.log(jnp.sum(jnp.exp(scores - row_max), axis=1, keepdims=True))
    loss_ref[...] = log_total - jnp.sum(scores * is_positive, axis=1, keepdims=True)
    weights = (jnp.exp(scores - log_total) - is_positive).astype(BF16)
    weights_ref[...] = weights
    for block, grad_ref in enumerate(grad_refs):
        grad_ref[...] = lax.dot_general(
            weights[:, block * block_rows : (block + 1) * block_rows],
            updated,
            (((0,), (0,)), ((), ())),
            preferred_element_type=F32,
        ).astype(BF16)


def finish_body(weights_ref, updated_ref, loss_ref, *refs):
    tool_refs, (grad_ref, result_ref, chain_loss_ref) = refs[:-3], refs[-3:]
    result_ref[...] = updated_ref[...]
    chain_loss_ref[...] = loss_ref[...]
    block_rows = tool_refs[0].shape[0]
    grad_ref[...] = sum(
        jnp.dot(
            weights_ref[:, j * block_rows : (j + 1) * block_rows], ref[...], preferred_element_type=F32
        )
        for j, ref in enumerate(tool_refs)
    )


def weight_pieces(own, own_later, groups, hold, asked):
    near = moved(own, (0, 0, 1), (1, 1, 8))
    near_y = moved(own_later, (0, 0, 2))
    first = after(near, asked)
    near, near_y = hold(near, near_y)
    turned = moved(first, (0, 0, 2), (1, 1, 1))
    far_y = moved(first, (1, 1, 2))
    far_both = moved(turned, (1, 1, 2))
    levels = []
    for level in range(16, groups, 16):
        base = moved(own, (0, 0, level), (1, 1, level ^ 8))
        by_x, by_y = (moved(base, (0, 0, bit), (1, 1, bit)) for bit in (1, 2))
        both = moved(by_x, (0, 0, 2), (1, 1, 2))
        levels += [(level ^ m, shard, level ^ 8 ^ m) for m, shard in enumerate((base, by_x, by_y, both))]
    return [(1, near, 8), (3, turned, 9), *levels], (near_y, far_y, far_both)


def shared_pieces(own, symmetric, exchanged, near_y, far_y, far_both, later, last):
    pieces = [(0, own, 0, own)]
    for (mask, shard, other_mask), given in zip(symmetric, exchanged):
        pieces += [(mask, shard, other_mask, shard), (other_mask, given, mask, given)]
    pieces.append((2, near_y, 2, flipped(after(near_y, later), "dp", 1)))
    pieces.append((10, flipped(after(far_y, later), "dp", 1), 10, far_y))
    pieces.append((11, flipped(after(far_both, last), "dp", 1), 11, far_both))
    return pieces


def local(
    queries,
    first_owner,
    first_row,
    tool_table,
    norm_gain,
    weight_in,
    bias_in,
    weight_out,
    bias_out,
    tool_embeds,
    positive,
):
    chains, features = queries.shape
    groups, cycle = lax.axis_size("mp"), lax.axis_size("dp")
    capacity = 2 * chains // groups
    slots = groups * capacity
    units = weight_in.shape[0]
    block_rows = tool_embeds.shape[0]
    tool_count = block_rows * cycle

    def whole(shape, dtype):
        return jax.ShapeDtypeStruct(shape, dtype)

    owner_row = first_owner.reshape(1, chains)
    width = -(-(units + capacity) // 128) * 128
    message = kernel_call(
        functools.partial(request_body, capacity),
        whole((groups, 1, width), F32),
        owner_row,
        first_row.reshape(1, chains),
        bias_in,
    )
    asked = lax.all_to_all(message, "mp", split_axis=0, concat_axis=0, tiled=True)
    served = kernel_call(
        functools.partial(serve_body, capacity, units),
        whole((slots, features), BF16),
        asked,
        tool_table,
    )
    packed = kernel_call(
        functools.partial(pack_body, capacity, groups),
        whole((chains + TILE_ROWS, features), BF16),
        after(owner_row, served),
        positive.reshape(1, chains),
        norm_gain,
        bias_out,
        queries,
    )
    own = jnp.concatenate([weight_in, weight_out], axis=0)
    own_later = after(own, message)
    held = []

    def hold(*early):
        early_and_served = lax.optimization_barrier((*early, served))
        held.append(early_and_served[-1])
        return early_and_served[:-1]

    symmetric, single = weight_pieces(own, own_later, groups, hold, asked)
    fetched = lax.all_to_all(held[0], "mp", split_axis=0, concat_axis=0, tiled=True)
    exchanged = [flipped(after(shard, packed), "dp", 1) for _, shard, _ in symmetric]
    shifted, normed, positive_row = kernel_call(
        select_body,
        (whole((chains, features), F32), whole((chains, features), BF16), whole((1, chains), jnp.int32)),
        packed,
        after(fetched, exchanged[0]),
    )

    neighbour_normed = flipped(normed, "mp", 4)
    pieces = shared_pieces(own, symmetric, exchanged, *single, normed, neighbour_normed)
    early = (own, symmetric[0][1], exchanged[0])

    def hidden(rows, some, held_as, *so_far):
        shards = []
        for piece in some:
            for shard in (piece[1], piece[3]):
                if all(shard is not s for s in shards):
                    shards.append(shard)
        index_of = {id(s): i for i, s in enumerate(shards)}
        plan = tuple((mask, index_of[id(s)], other, index_of[id(t)]) for mask, s, other, t in some)
        first = 2 + len(so_far)
        return kernel_call(
            functools.partial(hidden_body, plan, len(so_far)),
            whole((chains, features), held_as),
            rows,
            asked,
            *so_far,
            *(pltpu.with_memory_space_constraint(s, pltpu.HBM) if any(s is e for e in early) else s for s in shards),
            in_place=range(first, first + len(shards)),
            scratch=(
                pltpu.VMEM((len(plan) * units, features), BF16),
                pltpu.VMEM((len(plan) * units, features), BF16),
                pltpu.SemaphoreType.DMA((2, len(plan))),
            ),
            vmem=LARGE_VMEM,
        )

    neighbour = hidden(
        neighbour_normed, pieces[-1:], BF16, hidden(neighbour_normed, pieces[:-1], F32)
    )
    total = hidden(after(normed, neighbour), pieces, F32)
    late_tools = after(tool_embeds, neighbour)
    tools = [tool_embeds] + [flipped(late_tools, "dp", j) for j in range(1, cycle)]
    updated, loss, weights, *grads = kernel_call(
        functools.partial(score_body, cycle),
        (
            whole((chains, features), BF16),
            whole((chains, 1), F32),
            whole((chains, tool_count), BF16),
            *(whole((block_rows, features), BF16) for _ in range(cycle)),
        ),
        shifted,
        total,
        flipped(neighbour, "mp", 4),
        positive_row,
        *tools,
    )
    query_grad, updated, loss = kernel_call(
        finish_body,
        (whole((chains, features), F32), whole((chains, features), BF16), whole((chains, 1), F32)),
        weights,
        updated,
        loss,
        *tools,
    )

    grad = grads[0].astype(F32)
    for block in range(1, cycle):
        grad = grad + flipped(grads[block], "dp", block).astype(F32)
    bits = [1 << b for b in range((groups - 1).bit_length())]
    turned = bits[len(bits) // 2 :] + bits[: len(bits) // 2]
    for bit, other_bit in zip(bits, turned):
        rounded = grad.astype(BF16)
        grad = rounded.astype(F32) + moved(rounded, (0, 0, bit), (1, 1, other_bit)).astype(F32)
    grad_scale = (tool_count / (chains * groups * cycle)) ** 0.5
    return updated, loss[:, 0], query_grad, grad * grad_scale


def solution(mesh):
    in_specs = (
        P(("dp", "mp"), None),
        P(("dp", "mp"), None),
        P(("dp", "mp")),
        P("mp", None),
        P(),
        P("mp", None),
        P("mp"),
        P("mp", None),
        P(),
        P("dp", None),
        P(("dp", "mp")),
    )
    out_specs = (P(("dp", "mp"), None), P(("dp", "mp")), P(("dp", "mp"), None), P("dp", None))
    return jax.shard_map(local, mesh=mesh, in_specs=in_specs, out_specs=out_specs, check_vma=False)
```

```python
import functools

import jax
import jax.numpy as jnp
from jax import lax
from jax.experimental import pallas as pl
from jax.experimental.pallas import tpu as pltpu
from jax.sharding import PartitionSpec as P

F32 = jnp.float32
BF16 = jnp.bfloat16
DIGIT = 256
TILE_ROWS = 16
SMALL_VMEM = 6 * 1024 * 1024
LARGE_VMEM = 14 * 1024 * 1024


def flipped(block, axis, mask):
    return lax.ppermute(block, axis, [(i, i ^ mask) for i in range(lax.axis_size(axis))])


def moved(block, *moves):
    cycle, groups = lax.axis_size("dp"), lax.axis_size("mp")
    route = [
        ((d ^ to ^ source) * groups + (i ^ mask), d * groups + i)
        for to, source, mask in moves
        for d in range(to, cycle, 2)
        for i in range(groups)
    ]
    return lax.ppermute(block, ("dp", "mp"), route)


def after(value, *others):
    return lax.optimization_barrier((value, *others))[0]


def kernel_call(body, out_shape, *args, in_place=(), scratch=(), vmem=SMALL_VMEM):
    return pl.pallas_call(
        body,
        out_shape=out_shape,
        in_specs=[
            pl.BlockSpec(memory_space=pltpu.HBM if i in in_place else pltpu.VMEM) for i in range(len(args))
        ],
        out_specs=jax.tree.map(lambda _: pl.BlockSpec(memory_space=pltpu.VMEM), out_shape),
        scratch_shapes=scratch,
        compiler_params=pltpu.CompilerParams(vmem_limit_bytes=vmem),
    )(*args)


def iota(shape, dimension):
    return lax.broadcasted_iota(jnp.int32, shape, dimension)


def slots_of(owner, groups):
    chains = owner.shape[1]
    marks = (owner == iota((groups, chains), 0)).astype(F32)
    before = (iota((chains, chains), 0) < iota((chains, chains), 1)).astype(BF16)
    counts = jnp.dot(marks.astype(BF16), before, preferred_element_type=F32)
    return marks, jnp.sum(counts * marks, axis=0, keepdims=True)


def request_body(capacity, owner_ref, row_ref, bias_ref, message_ref):
    groups, _, width = message_ref.shape
    bias_count = bias_ref.shape[0]
    marks, rank = slots_of(owner_ref[...], groups)
    ranked = (rank.astype(jnp.int32) == iota((capacity, rank.shape[1]), 0)).astype(F32) * row_ref[...].astype(F32)
    request = lax.dot_general(
        marks.astype(BF16), ranked.astype(BF16), (((1,), (1,)), ((), ())), preferred_element_type=F32
    )
    bias = jnp.broadcast_to(bias_ref[...].astype(F32)[None, :], (groups, bias_count))
    rest = jnp.zeros((groups, width - bias_count - capacity), F32)
    message_ref[...] = jnp.concatenate([bias, request, rest], axis=1).reshape(message_ref.shape)


def serve_body(capacity, bias_count, message_ref, table_ref, rows_ref):
    groups = message_ref.shape[0]
    slots, held = groups * capacity, table_ref.shape[0]
    message = message_ref[...].reshape(groups, message_ref.shape[2])
    wanted = message[:, bias_count : bias_count + capacity].astype(BF16)
    spread = (iota((slots, groups), 0) // capacity == iota((slots, groups), 1)).astype(BF16)
    by_rank = jnp.dot(spread, wanted, preferred_element_type=F32)
    mine = (iota((slots, capacity), 0) % capacity == iota((slots, capacity), 1)).astype(F32)
    row = jnp.sum(by_rank * mine, axis=1, keepdims=True).astype(jnp.int32)
    pick = (row == iota((slots, held), 1)).astype(BF16)
    rows_ref[...] = jnp.dot(pick, table_ref[...], preferred_element_type=F32).astype(BF16)


def pack_body(capacity, groups, owner_ref, positive_ref, gain_ref, bias_ref, queries_ref, packed_ref):
    chains, features = queries_ref.shape
    owner, positive = owner_ref[...], positive_ref[...]
    _, rank = slots_of(owner, groups)
    slot = owner * capacity + rank.astype(jnp.int32)
    small = jnp.concatenate([slot, positive // DIGIT, positive % DIGIT], axis=0).astype(F32)
    small = jnp.concatenate([small, jnp.zeros((3, features - chains), F32)], axis=1)
    wide = jnp.concatenate([ref[...].astype(F32)[None, :] for ref in (gain_ref, bias_ref)], axis=0)
    rest = jnp.zeros((TILE_ROWS - 5, features), F32)
    packed_ref[:chains, :] = queries_ref[...]
    packed_ref[chains:, :] = jnp.concatenate([small, wide, rest], axis=0).astype(BF16)


def select_body(packed_ref, fetched_ref, shifted_ref, normed_ref, positive_ref):
    slots = fetched_ref.shape[0]
    chains = shifted_ref.shape[0]
    extra = packed_ref[chains:, :].astype(F32)
    digits = extra[:3, :chains].astype(jnp.int32)
    positive_ref[...] = digits[1:2, :] * DIGIT + digits[2:3, :]
    pick = (digits[0:1, :] == iota((slots, chains), 0)).astype(F32).T.astype(BF16)
    rows = jnp.dot(pick, fetched_ref[...], preferred_element_type=F32)
    combined = packed_ref[:chains, :].astype(F32) + rows
    centred = combined - jnp.mean(combined, axis=1, keepdims=True)
    spread = jnp.mean(centred * centred, axis=1, keepdims=True)
    normed_ref[...] = (centred * lax.rsqrt(spread + 1e-05) * extra[3:4, :]).astype(BF16)
    shifted_ref[...] = combined + extra[4:5, :]


def gelu(u):
    return 0.5 * u * (1.0 + jnp.tanh(0.7978845608028654 * (u + 0.044715 * (u * u * u))))


def hidden_body(plan, continued, normed_ref, message_ref, *refs):
    sums, shards, (total_ref, held_in, held_out, sems) = refs[:continued], refs[continued:-4], refs[-4:]
    units = held_in.shape[0] // len(plan)
    me, first_core = lax.axis_index("mp"), lax.axis_index("dp") % 2 == 0
    held = (held_in, held_out)

    def copy(at, p, side):
        return pltpu.make_async_copy(
            shards[at].at[pl.ds(side * units, units)], held[side].at[pl.ds(p * units, units)], sems.at[side, p]
        )

    for side in (0, 1):
        for p, (_, at, _, other_at) in enumerate(plan):
            if at == other_at:
                copy(at, p, side).start()
            else:

                @pl.when(first_core)
                def _():
                    copy(at, p, side).start()

                @pl.when(jnp.logical_not(first_core))
                def _():
                    copy(other_at, p, side).start()

    normed = normed_ref[...]
    places = [me ^ jnp.where(first_core, mask, other_mask) for mask, _, other_mask, _ in plan]
    bias = jnp.concatenate(
        [message_ref[pl.ds(place, 1)].reshape(1, message_ref.shape[2])[:, :units] for place in places], axis=1
    )
    for p, (_, at, _, _) in enumerate(plan):
        copy(at, p, 0).wait()
    preact = lax.dot_general(normed, held_in[...], (((1,), (1,)), ((), ())), preferred_element_type=F32)
    activated = gelu(preact + bias).astype(BF16)
    for p, (_, at, _, _) in enumerate(plan):
        copy(at, p, 1).wait()
    total = jnp.dot(activated, held_out[...], preferred_element_type=F32)
    for sum_ref in sums:
        total = total + sum_ref[...]
    total_ref[...] = total.astype(total_ref.dtype)


def score_body(
    blocks,
    shifted_ref,
    total_ref,
    other_ref,
    positive_ref,
    *refs,
):
    tools = [ref[...] for ref in refs[:blocks]]
    updated_ref, loss_ref, weights_ref, *grad_refs = refs[blocks:]
    block_rows = tools[0].shape[0]
    branch = total_ref[...] + other_ref[...].astype(F32)
    updated = (shifted_ref[...] + branch).astype(BF16)
    updated_ref[...] = updated
    scores = jnp.concatenate(
        [
            lax.dot_general(updated, t, (((1,), (1,)), ((), ())), preferred_element_type=F32)
            for t in tools
        ],
        axis=1,
    )
    tool = iota((scores.shape[1], scores.shape[0]), 0)
    column = ((tool // block_rows) ^ lax.axis_index("dp")) * block_rows + tool % block_rows
    is_positive = (column == positive_ref[...]).astype(F32).T
    row_max = jnp.max(scores, axis=1, keepdims=True)
    log_total = row_max + jnp.log(jnp.sum(jnp.exp(scores - row_max), axis=1, keepdims=True))
    loss_ref[...] = log_total - jnp.sum(scores * is_positive, axis=1, keepdims=True)
    weights = (jnp.exp(scores - log_total) - is_positive).astype(BF16)
    weights_ref[...] = weights
    for block, grad_ref in enumerate(grad_refs):
        grad_ref[...] = lax.dot_general(
            weights[:, block * block_rows : (block + 1) * block_rows],
            updated,
            (((0,), (0,)), ((), ())),
            preferred_element_type=F32,
        ).astype(BF16)


def finish_body(weights_ref, updated_ref, loss_ref, *refs):
    tool_refs, (grad_ref, result_ref, chain_loss_ref) = refs[:-3], refs[-3:]
    result_ref[...] = updated_ref[...]
    chain_loss_ref[...] = loss_ref[...]
    block_rows = tool_refs[0].shape[0]
    grad_ref[...] = sum(
        jnp.dot(
            weights_ref[:, j * block_rows : (j + 1) * block_rows], ref[...], preferred_element_type=F32
        )
        for j, ref in enumerate(tool_refs)
    )


def weight_pieces(own, own_later, groups, hold, asked):
    near = moved(own, (0, 0, 1), (1, 1, 8))
    near_y = moved(own_later, (0, 0, 2), (1, 1, 0))
    first = after(near, asked)
    near, near_y = hold(near, near_y)
    turned = moved(first, (0, 0, 2), (1, 1, 1))
    far_y = moved(first, (1, 1, 2))
    far_both = moved(turned, (1, 1, 2))
    levels = []
    for level in range(16, groups, 16):
        base = moved(own, (0, 0, level), (1, 1, level ^ 8))
        by_x, by_y = (moved(base, (0, 0, bit), (1, 1, bit)) for bit in (1, 2))
        both = moved(by_x, (0, 0, 2), (1, 1, 2))
        levels += [(level ^ m, shard, level ^ 8 ^ m) for m, shard in enumerate((base, by_x, by_y, both))]
    return [(1, near, 8), (3, turned, 9), *levels], (near_y, far_y, far_both)


def shared_pieces(own, symmetric, exchanged, near_y, far_y, far_both, later, last):
    pieces = [(0, own, 0, own)]
    for (mask, shard, other_mask), given in zip(symmetric, exchanged):
        pieces += [(mask, shard, other_mask, shard), (other_mask, given, mask, given)]
    pieces.append((2, near_y, 2, flipped(after(near_y, later), "dp", 1)))
    pieces.append((10, flipped(after(far_y, later), "dp", 1), 10, far_y))
    pieces.append((11, flipped(after(far_both, last), "dp", 1), 11, far_both))
    return pieces


def local(
    queries,
    first_owner,
    first_row,
    tool_table,
    norm_gain,
    weight_in,
    bias_in,
    weight_out,
    bias_out,
    tool_embeds,
    positive,
):
    chains, features = queries.shape
    groups, cycle = lax.axis_size("mp"), lax.axis_size("dp")
    capacity = 2 * chains // groups
    slots = groups * capacity
    units = weight_in.shape[0]
    block_rows = tool_embeds.shape[0]
    tool_count = block_rows * cycle

    def whole(shape, dtype):
        return jax.ShapeDtypeStruct(shape, dtype)

    owner_row = first_owner.reshape(1, chains)
    width = -(-(units + capacity) // 128) * 128
    message = kernel_call(
        functools.partial(request_body, capacity),
        whole((groups, 1, width), F32),
        owner_row,
        first_row.reshape(1, chains),
        bias_in,
    )
    asked = lax.all_to_all(message, "mp", split_axis=0, concat_axis=0, tiled=True)
    served = kernel_call(
        functools.partial(serve_body, capacity, units),
        whole((slots, features), BF16),
        asked,
        tool_table,
    )
    packed = kernel_call(
        functools.partial(pack_body, capacity, groups),
        whole((chains + TILE_ROWS, features), BF16),
        after(owner_row, served),
        positive.reshape(1, chains),
        norm_gain,
        bias_out,
        queries,
    )
    own = jnp.concatenate([weight_in, weight_out], axis=0)
    own_later = after(own, message)
    held = []

    def hold(*early):
        early_and_served = lax.optimization_barrier((*early, served))
        held.append(early_and_served[-1])
        return early_and_served[:-1]

    symmetric, single = weight_pieces(own, own_later, groups, hold, asked)
    fetched = lax.all_to_all(held[0], "mp", split_axis=0, concat_axis=0, tiled=True)
    exchanged = [flipped(after(shard, packed), "dp", 1) for _, shard, _ in symmetric]
    shifted, normed, positive_row = kernel_call(
        select_body,
        (whole((chains, features), F32), whole((chains, features), BF16), whole((1, chains), jnp.int32)),
        packed,
        after(fetched, exchanged[0]),
    )

    neighbour_normed = flipped(normed, "mp", 4)
    pieces = shared_pieces(own, symmetric, exchanged, *single, normed, neighbour_normed)
    early = (own, symmetric[0][1], exchanged[0])

    def hidden(rows, some, held_as, *so_far):
        shards = []
        for piece in some:
            for shard in (piece[1], piece[3]):
                if all(shard is not s for s in shards):
                    shards.append(shard)
        index_of = {id(s): i for i, s in enumerate(shards)}
        plan = tuple((mask, index_of[id(s)], other, index_of[id(t)]) for mask, s, other, t in some)
        first = 2 + len(so_far)
        return kernel_call(
            functools.partial(hidden_body, plan, len(so_far)),
            whole((chains, features), held_as),
            rows,
            asked,
            *so_far,
            *(pltpu.with_memory_space_constraint(s, pltpu.HBM) if any(s is e for e in early) else s for s in shards),
            in_place=range(first, first + len(shards)),
            scratch=(
                pltpu.VMEM((len(plan) * units, features), BF16),
                pltpu.VMEM((len(plan) * units, features), BF16),
                pltpu.SemaphoreType.DMA((2, len(plan))),
            ),
            vmem=LARGE_VMEM,
        )

    neighbour = hidden(
        neighbour_normed, pieces[-1:], BF16, hidden(neighbour_normed, pieces[:-1], F32)
    )
    total = hidden(after(normed, neighbour), pieces, F32)
    late_tools = after(tool_embeds, neighbour)
    tools = [tool_embeds] + [flipped(late_tools, "dp", j) for j in range(1, cycle)]
    updated, loss, weights, *grads = kernel_call(
        functools.partial(score_body, cycle),
        (
            whole((chains, features), BF16),
            whole((chains, 1), F32),
            whole((chains, tool_count), BF16),
            *(whole((block_rows, features), BF16) for _ in range(cycle)),
        ),
        shifted,
        total,
        flipped(neighbour, "mp", 4),
        positive_row,
        *tools,
    )
    query_grad, updated, loss = kernel_call(
        finish_body,
        (whole((chains, features), F32), whole((chains, features), BF16), whole((chains, 1), F32)),
        weights,
        updated,
        loss,
        *tools,
    )

    grad = grads[0].astype(F32)
    for block in range(1, cycle):
        grad = grad + flipped(grads[block], "dp", block).astype(F32)
    bits = [1 << b for b in range((groups - 1).bit_length())]
    turned = bits[len(bits) // 2 :] + bits[: len(bits) // 2]
    for bit, other_bit in zip(bits, turned):
        rounded = grad.astype(BF16)
        grad = rounded.astype(F32) + moved(rounded, (0, 0, bit), (1, 1, other_bit)).astype(F32)
    grad_scale = (tool_count / (chains * groups * cycle)) ** 0.5
    return updated, loss[:, 0], query_grad, grad * grad_scale


def solution(mesh):
    in_specs = (
        P(("dp", "mp"), None),
        P(("dp", "mp"), None),
        P(("dp", "mp")),
        P("mp", None),
        P(),
        P("mp", None),
        P("mp"),
        P("mp", None),
        P(),
        P("dp", None),
        P(("dp", "mp")),
    )
    out_specs = (P(("dp", "mp"), None), P(("dp", "mp")), P(("dp", "mp"), None), P("dp", None))
    return jax.shard_map(local, mesh=mesh, in_specs=in_specs, out_specs=out_specs, check_vma=False)
```
